128 devices in a mesh: bx: 8 (over x, core), by: 16 (over z, y).
Axes of the slice: x: 4, y: 4, z: 4, core: 2. Of those that a mesh axis runs over, the one named last changes fastest.
Arguments:
- features: bfloat16 [1024, 8, 8, 512], P(('bx', 'by')), may hold values from -6 to 6
- neighbour_ids: int32 [1024, 27], P(('bx', 'by')), may hold values from -1 to 1023, as said below
- conv_weight: bfloat16 [27, 64, 64], replicated, may hold values from -0.15625 to 0.15625
- conv_bias: float32 [64], replicated, may hold values from -3 to 3
- down_weight: bfloat16 [8, 64, 128], replicated, may hold values from -0.25 to 0.25
- coarse_owner: int32 [1024, 1], P(('bx', 'by')), may hold values from 0 to 15; in each aligned block of 8 rows (0 to 7, 8 to 15, ...) at most 2 rows name the same one
Outputs:
- coarse_bricks: bfloat16 [4096, 4, 4, 512], P(('bx', 'by'))
The draws below stay inside these ranges and needn't reach their ends.
Inputs may be any that keep to these rules, and one draw needn't show every extreme that they name: `neighbour_ids`: entry 13 of each brick is the brick itself. Every other entry (sx+1)*9+(sy+1)*3+(sz+1) of a brick on device (i, j) is -1 or a brick on a device whose bx index is i or i+sx and whose by index is j or j+sy. `coarse_owner`: among the bricks of one device, at most 2 have the same owner.
All inputs are finite; a program needn't handle non-finite values.
Results may differ from the reference program's by a relative error of at most 0.0049.
Values may be sent and summed in bfloat16 or wider, within the bound.
A program may use at most 64 MiB of HBM per device.

```python
import math
import jax
import jax.numpy as jnp
import numpy as np
from jax import lax

EDGE = 8
CH = 64
CO = 128
B_DEV = 8
CAP = 2
BRICKS = 1024
ROWS = 4096
N_BX = 8
N_BY = 16


def draw_neighbour_ids(key, part):
    key = jax.random.fold_in(key, 11)
    keys = jax.random.split(key, 4)
    bricks = jnp.arange(BRICKS, dtype=jnp.int32)[:, None]
    device = bricks // B_DEV
    index_x = device // N_BY
    index_y = device % N_BY
    taps = jnp.arange(27, dtype=jnp.int32)[None, :]
    step_x = taps // 9 - 1
    step_y = taps // 3 % 3 - 1
    moved_x = index_x + step_x * jax.random.randint(keys[0], (BRICKS, 27), 0, 2)
    moved_y = index_y + step_y * jax.random.randint(keys[1], (BRICKS, 27), 0, 2)
    moved_x = jnp.where((moved_x < 0) | (moved_x >= N_BX), index_x, moved_x)
    moved_y = jnp.where((moved_y < 0) | (moved_y >= N_BY), index_y, moved_y)
    slots = jax.random.randint(keys[2], (BRICKS, 27), 0, B_DEV)
    present = jax.random.randint(keys[3], (BRICKS, 27), 0, 10) < 7
    target = (moved_x * N_BY + moved_y) * B_DEV + slots
    target = jnp.where(present, target, -1)
    target = jnp.where(taps == 13, bricks, target)
    target = target.at[0, 0].set(-1)
    return target.astype(jnp.int32)


def shard_levels(own_key, extent, shards, low, largest):
    loudness, own = 1.0, jax.random.fold_in(own_key, 6)
    for position, blocks in shards:
        draws = jnp.exp(jax.random.uniform(jax.random.fold_in(own, position), (blocks,), jnp.float32, low / len(shards), largest / len(shards)))
        loudness = loudness * jnp.repeat(draws, extent[position] // blocks).reshape([-1 if axis == position else 1 for axis in range(len(extent))])
    return loudness


def shared_out(stream_key, own, number, rows, amount, top, bound, skew):
    sequence = jax.random.permutation(stream_key, amount)
    heavy_load, common = shares(amount, rows * top, bound, skew, True), shares(amount, rows * top, bound, skew, False)
    places = jnp.arange(amount)

    def named(tallies, turn):
        used = int((tallies > 0).sum())
        fixed = max(1, used // 4)
        passed = fixed + (places - fixed + turn * (used - fixed)) % max(1, amount - fixed)
        return jnp.zeros((amount,), jnp.int32).at[sequence[jnp.where(places < fixed, places, passed)]].set(jnp.asarray(tallies, jnp.int32))

    tallies = jnp.where(number % 4 == 0, named(heavy_load, number // 4), named(common, number - number // 4 - 1))
    mixed = jax.random.permutation(jax.random.fold_in(own, 3), amount)
    source_of, receiver = mixed[0:amount // 2 * 2:2], mixed[1:amount // 2 * 2:2]
    margin = jnp.minimum(tallies[source_of] - 1, bound - tallies[receiver]) // 2
    margin = jnp.where((source_of == sequence[0]) | (receiver == sequence[0]) | (tallies[receiver] == 0), 0, jnp.maximum(margin, 0))
    passed = jax.random.randint(jax.random.fold_in(own, 4), (amount // 2,), 0, 1 << 20) % (margin + 1)
    tallies = tallies.at[source_of].add(-passed).at[receiver].add(passed)
    items = jnp.searchsorted(jnp.cumsum(tallies), jnp.arange(rows * top), side="right").astype(jnp.int32)
    listing = items.reshape(top, rows).T
    listing = listing[jax.random.permutation(jax.random.fold_in(own, 1), rows)]
    turn = jax.random.randint(jax.random.fold_in(own, 2), (rows, 1), 0, top)
    return jnp.take_along_axis(listing, (jnp.arange(top)[None, :] + turn) % top, axis=1)


def shares(number_of, total, most, skew, full):
    portions = [(1 << 20) // math.isqrt(rank ** skew) + 1 for rank in range(1, number_of + 1)]
    largest = most if full else min(most, max(-(-total // number_of), total * portions[0] // sum(portions)))
    least = 1 if total - largest >= number_of - 1 else 0
    given, spare = [largest] + [least] * (number_of - 1), total - largest - least * (number_of - 1)
    while spare > 0:
        candidates = [i for i in range(1, number_of) if given[i] < largest] or [i for i in range(1, number_of) if given[i] < most]
        pool, left = sum([portions[i] for i in candidates]), spare
        for i in candidates:
            more = min(most - given[i], max(1, left * portions[i] // pool), spare)
            given[i] = given[i] + more
            spare = spare - more
    return np.array(given)


def noise(stream_key, shape, width, most, pieces=(), kind=jnp.bfloat16):
    array = width * jax.random.normal(stream_key, shape, jnp.float32)
    if pieces:
        array = array * shard_levels(stream_key, shape, pieces, -0.22, 0.18)
    return jnp.clip(array, -most, most).astype(kind)


def setup_inputs(seed: int = 0) -> dict:
    seeds = jax.random.split(jax.random.key(seed), 7)
    features = noise(seeds[0], (BRICKS, EDGE, EDGE, EDGE * CH), 1.0, 6.0, ((0, 128),))
    neighbour_ids = draw_neighbour_ids(jax.random.fold_in(seeds[6], 71), 0)
    conv_weight = noise(seeds[2], (27, CH, CH), (27 * CH) ** -0.5, 0.15625)
    conv_bias = noise(seeds[3], (CH,), 0.5, 3.0, (), jnp.float32)
    down_weight = noise(seeds[4], (8, CH, CO), (8 * CH) ** -0.5, 0.25)
    coarse_owner_keys = jax.random.split(jax.random.fold_in(seeds[5], 1), BRICKS // B_DEV)
    coarse_owner_turns = jax.random.permutation(jax.random.fold_in(seeds[5], 3), BRICKS // B_DEV)
    coarse_owner = jax.vmap(lambda own, number: shared_out(jax.random.fold_in(seeds[5], 2), own, number, B_DEV, N_BY, 1, CAP, 2))(coarse_owner_keys, coarse_owner_turns).reshape((BRICKS, 1))
    return dict(features=features, neighbour_ids=neighbour_ids, conv_weight=conv_weight, conv_bias=conv_bias, down_weight=down_weight, coarse_owner=coarse_owner)


offsets = (-1, 0, 1)


def layer_slice(step):
    if step < 0:
        return slice(7, 8)
    if step == 0:
        return slice(0, 8)
    return slice(0, 1)


def padded_block(cells_all, block_ids):
    plane_x = []
    for shift_x in offsets:
        plane_y = []
        for shift_y in offsets:
            plane_z = []
            for shift_z in offsets:
                column = block_ids[:, (shift_x + 1) * 9 + (shift_y + 1) * 3 + (shift_z + 1)]
                taken = jnp.take(cells_all, jnp.maximum(column, 0), axis=0)
                taken = taken[:, layer_slice(shift_x), layer_slice(shift_y), layer_slice(shift_z)]
                taken = jnp.where((column >= 0)[:, None, None, None, None], taken, jnp.zeros((), taken.dtype))
                plane_z.append(taken)
            plane_y.append(jnp.concatenate(plane_z, 3))
        plane_x.append(jnp.concatenate(plane_y, 2))
    return jnp.concatenate(plane_x, 1)


def reference(features, neighbour_ids, conv_weight, conv_bias, down_weight, coarse_owner):
    cells_all = features.reshape(BRICKS, EDGE, EDGE, EDGE, CH)
    device_count = N_BX * N_BY

    def one_block(inputs):
        block_ids, own = inputs
        padded = padded_block(cells_all, block_ids)
        total = jnp.zeros((B_DEV * EDGE**3, CH), jnp.float32)
        for tap_x in range(3):
            for tap_y in range(3):
                for tap_z in range(3):
                    window = padded[:, tap_x:tap_x + EDGE, tap_y:tap_y + EDGE, tap_z:tap_z + EDGE].reshape(-1, CH)
                    total = total + jnp.dot(window, conv_weight[tap_x * 9 + tap_y * 3 + tap_z], preferred_element_type=jnp.float32)
        own_f = own.reshape(-1, CH).astype(jnp.float32)
        hidden = (own_f + jax.nn.silu(total + conv_bias[None, :])).astype(jnp.bfloat16)
        half = EDGE // 2
        split = hidden.reshape(B_DEV, half, 2, half, 2, half, 2, CH).astype(jnp.float32)
        kernel = down_weight.reshape(2, 2, 2, CH, CO).astype(jnp.float32)
        coarse = jnp.einsum("nxaybzcj,abcjo->nxyzo", split, kernel)
        return coarse.astype(jnp.bfloat16).reshape(B_DEV, half, half, half * CO)

    coarse_all = lax.map(one_block, (neighbour_ids.reshape(device_count, B_DEV, 27), cells_all.reshape(device_count, B_DEV, EDGE, EDGE, EDGE, CH)))
    coarse_all = coarse_all.reshape(BRICKS, EDGE // 2, EDGE // 2, (EDGE // 2) * CO)
    owners = coarse_owner[:, 0].astype(jnp.int32)
    onehot = (owners.reshape(device_count, B_DEV)[:, :, None] == jnp.arange(N_BY, dtype=jnp.int32)[None, None, :]).astype(jnp.int32)
    ranks = jnp.sum((jnp.cumsum(onehot, axis=1) - onehot) * onehot, axis=2).reshape(BRICKS)
    bricks = jnp.arange(BRICKS, dtype=jnp.int32)
    device = bricks // B_DEV
    index_x = device // N_BY
    index_y = device % N_BY
    target = ((index_x * N_BY + owners) * N_BY + index_y) * CAP + ranks
    result = jnp.zeros((ROWS, EDGE // 2, EDGE // 2, (EDGE // 2) * CO), jnp.bfloat16)
    return result.at[target.astype(jnp.int32)].set(coarse_all)
```

```python
import functools

import jax
import jax.numpy as jnp
from jax import lax
from jax.experimental import pallas as pl
from jax.experimental.pallas import tpu as pltpu
from jax.sharding import PartitionSpec as P

MESH = pl.DeviceIdType.MESH
F32 = jnp.float32
BF16 = jnp.bfloat16

EDGE = 8
BRICKS = 8
CH = 64
CO = 128
LANES = EDGE * CH
ROWS = BRICKS * EDGE * EDGE
HALF = 4 * CH
BAND = 6 * CH
FACE = BRICKS * EDGE
MESSAGE = FACE + 2 * BRICKS

T_FACE = BRICKS * EDGE
T_ZERO = T_FACE + 2 * BRICKS
T_SIZE = T_ZERO + EDGE
Y_ZERO = 2 * BRICKS
Y_SIZE = Y_ZERO + 1
E_ZERO = 4 * BRICKS
E_SIZE = E_ZERO + 1

STEPS = (-1, 0, 1)
HALO = [(1, 0), (-1, 0), (0, 1), (0, -1), (1, 1), (1, -1), (-1, 1), (-1, -1)]


def iota(shape, dim):
    return lax.broadcasted_iota(jnp.int32, shape, dim)


def picked_rows():
    row = iota((4 * MESSAGE, ROWS), 0)
    source = iota((4 * MESSAGE, ROWS), 1)
    part, inner = row // MESSAGE, row % MESSAGE
    brick, other = inner // EDGE, inner % EDGE
    face_x = brick * 64 + jnp.where(part == 0, 56, 0) + other
    face_y = inner * 8 + jnp.where(part == 2, 7, 0)
    face = jnp.where(part < 2, face_x, face_y)
    second = inner >= FACE + BRICKS
    edge_x = jnp.where(part == 0, 56, 0) + jnp.where(second, 0, 7)
    edge_y = jnp.where(part == 2, 7, 0) + jnp.where(second, 0, 56)
    edge = other * 64 + jnp.where(part < 2, edge_x, edge_y)
    target = jnp.where(inner < FACE, face, edge)
    return (target == source).astype(F32).astype(BF16)


def repeat_rows(target, corner, first, rows):
    for k in range(BRICKS):
        target[corner, first + k] = jnp.broadcast_to(rows[k : k + 1], (EDGE, LANES))


def kernel(
    size_x, size_y,
    ids_hbm, owner_hbm, feat_hbm, conv_hbm, bias_hbm, down_hbm,
    out_ref,
    ids, owner, feat, conv, bias, down,
    index, sendbuf, xy_recv, edge_recv, table, ytab, etab,
    stack, band, dband, place, hidden, stage,
    load_sem, halo_send, halo_recv, out_send, out_recv, own_sem,
):
    i = lax.axis_index("bx")
    j = lax.axis_index("by")

    def beside(step_x, step_y):
        return (lax.rem(i + step_x + size_x, size_x), lax.rem(j + step_y + size_y, size_y))

    barrier = pltpu.get_barrier_semaphore()
    others = [(sx, sy) for sx, sy in HALO if sx != 0]
    for sx, sy in others:
        pl.semaphore_signal(barrier, inc=1, device_id=beside(sx, sy), device_id_type=MESH)
    for d in range(1, size_y):
        pl.semaphore_signal(barrier, inc=1, device_id=beside(0, d), device_id_type=MESH)

    loads = [
        pltpu.make_async_copy(source, target, load_sem.at[k])
        for k, (source, target) in enumerate(
            [
                (feat_hbm, feat),
                (conv_hbm, conv),
                (ids_hbm, ids),
                (owner_hbm, owner),
                (bias_hbm, bias),
                (down_hbm, down),
            ]
        )
    ]
    for load in loads:
        load.start()

    pick = picked_rows()
    loads[0].wait()
    picked = jnp.dot(pick, feat[...], preferred_element_type=F32)
    packed = picked.astype(BF16)
    for k in range(4):
        sendbuf[k] = packed[k * MESSAGE : (k + 1) * MESSAGE]

    pl.semaphore_wait(barrier, len(others) + size_y - 1)
    copies = []
    for k, (sx, sy) in enumerate(HALO):
        if k < 4:
            source, target = sendbuf.at[k], xy_recv.at[k]
        else:
            source = sendbuf.at[(k - 4) // 2, pl.ds(FACE, 16)]
            target = edge_recv.at[k - 4]
        copy = pltpu.make_async_remote_copy(
            src_ref=source,
            dst_ref=target,
            send_sem=halo_send.at[k],
            recv_sem=halo_recv.at[k],
            device_id=beside(sx, sy),
            device_id_type=MESH,
        )
        copy.start()
        copies.append(copy)

    table[0:T_FACE] = feat[...].astype(F32).reshape(T_FACE, EDGE, LANES)
    table[T_ZERO:T_SIZE] = jnp.zeros((EDGE, EDGE, LANES), F32)
    for k in range(2):
        face = picked[(2 + k) * MESSAGE : (2 + k) * MESSAGE + FACE]
        ytab[k, 0:BRICKS] = face.reshape(BRICKS, EDGE, LANES)
        ytab[k, Y_ZERO] = jnp.zeros((EDGE, LANES), F32)
    for k in range(4):
        first = k // 2 * MESSAGE + FACE + k % 2 * BRICKS
        repeat_rows(etab, k, 0, picked[first : first + BRICKS])
        etab[k, E_ZERO] = jnp.zeros((EDGE, LANES), F32)

    loads[2].wait()
    for g in range(BRICKS):
        for tap in range(27):
            sx, sy = tap // 9 - 1, tap // 3 % 3 - 1
            value = ids[g, tap]
            brick = value & 7
            far_x = jnp.where(value >> 3 >> 4 == i, 0, 1)
            far_y = jnp.where((value >> 3) & 15 == j, 0, 1)
            if sx == 0 and sy == 0:
                row, zero = brick * EDGE, T_ZERO
            elif sy == 0:
                edge_x, side = (7, 0) if sx < 0 else (0, 1)
                row = jnp.where(far_x == 0, brick * EDGE + edge_x, T_FACE + side * BRICKS + brick)
                zero = T_ZERO
            elif sx == 0:
                row, zero = far_y * BRICKS + brick, Y_ZERO
            else:
                row, zero = far_x * 16 + far_y * 8 + brick, E_ZERO
            index[g, tap] = jnp.where(value >= 0, row, zero)

    loads[1].wait()
    empty = jnp.zeros((CH, CH), BF16)
    blank = jnp.zeros((CH, 2 * CH), BF16)
    for ty in range(3):
        for tx in range(3):
            w = [conv[tx * 9 + ty * 3 + tz] for tz in range(3)]
            pairs = {
                -1: jnp.concatenate([w[0], empty], 1),
                0: jnp.concatenate([w[1], w[0]], 1),
                1: jnp.concatenate([w[2], w[1]], 1),
                2: jnp.concatenate([empty, w[2]], 1),
            }
            for place_in, depth_in in enumerate((0, 1, 2, 3, 4, -1)):
                for q in range(2):
                    first = tx * BAND + place_in * CH
                    band[ty, first : first + CH, q * 128 : (q + 1) * 128] = pairs.get(
                        depth_in - 2 * q, blank
                    )
    loads[5].wait()
    for a in range(2):
        for z in range(4):
            for b in range(2):
                for half in range(2):
                    first = b * 256 + half * 128
                    block = down[a * 4 + b * 2 + z % 2] if z // 2 == half else blank
                    dband[a, z * CH : (z + 1) * CH, first : first + 128] = block

    loads[3].wait()
    owners = [owner[g, 0] for g in range(BRICKS)]
    slots = []
    for g in range(BRICKS):
        rank = jnp.int32(0)
        for earlier in range(g):
            rank = rank + jnp.where(owners[earlier] == owners[g], 1, 0)
        slots.append(owners[g] * 2 + rank)
    col = iota((16, 256), 1)
    xy = iota((16, 256), 0)
    slot_of = jnp.zeros((16, 256), jnp.int32)
    for g in range(BRICKS):
        slot_of = jnp.where(col // 8 % 8 == g, slots[g], slot_of)
    slot_of = jnp.where((col // 64 == xy // 4) & (col % 8 == xy % 4 * 2), slot_of, -1)
    for s in range(2 * size_y):
        place[s * 16 : (s + 1) * 16] = (slot_of == s).astype(F32).astype(BF16)

    loads[4].wait()
    for copy in copies:
        copy.wait()
    for k in range(2):
        over_x = xy_recv[k].astype(F32)
        over_y = xy_recv[2 + k].astype(F32)
        first = T_FACE + k * BRICKS
        table[first : first + BRICKS] = over_x[0:FACE].reshape(BRICKS, EDGE, LANES)
        ytab[k, BRICKS : 2 * BRICKS] = over_y[0:FACE].reshape(BRICKS, EDGE, LANES)
        for side in range(2):
            first = FACE + side * BRICKS
            repeat_rows(etab, side * 2 + k, 8, over_y[first : first + BRICKS])
            repeat_rows(etab, k * 2 + side, 16, over_x[first : first + BRICKS])
            diagonal = edge_recv[k * 2 + side].astype(F32)
            diagonal = diagonal[side * BRICKS : (side + 1) * BRICKS]
            repeat_rows(etab, k * 2 + side, 24, diagonal)

    low = iota((EDGE, 128), 1) < CH
    last_row = iota((EDGE, BAND), 0) == 7
    first_row = iota((EDGE, BAND), 0) == 0

    def halves(read, centre, minus, plus):
        c = read(centre, 0, LANES)
        m = read(minus, LANES - 128, LANES)
        p = read(plus, 0, 128)
        e0 = jnp.where(low, c[:, 256:384], m)
        e1 = jnp.where(low, p, c[:, 128:256])
        return (
            jnp.concatenate([c[:, 0:256], e0], 1),
            jnp.concatenate([c[:, 256:512], e1], 1),
        )

    def one_slab(g, x):
        sx = -1 if x < 0 else (1 if x > 7 else 0)
        shift = x if sx == 0 else 0
        result = []
        for sy in STEPS:
            tap = (sx + 1) * 9 + (sy + 1) * 3
            if sy == 0:
                def read(row, low_lane, high_lane):
                    return table[row + shift, :, low_lane:high_lane]
            elif sx == 0:
                def read(row, low_lane, high_lane, side=(sy + 1) // 2):
                    lines = ytab[side, row, :, low_lane:high_lane]
                    return pltpu.roll(lines, (7 - x if side == 0 else 0 - x) & 7, 0)
            else:
                def read(row, low_lane, high_lane, corner=(sx + 1) // 2 * 2 + (sy + 1) // 2):
                    return etab[corner, row, :, low_lane:high_lane]
            result.append(halves(read, index[g, tap + 1], index[g, tap], index[g, tap + 2]))
        before, same, after = result
        return [
            [jnp.where(last_row, before[h], same[h]), same[h], jnp.where(first_row, after[h], same[h])]
            for h in range(2)
        ]

    def gather(pair, carry):
        for x in range(-1, 9):
            even = one_slab(pair * 2, x)
            odd = one_slab(pair * 2 + 1, x)
            for h in range(2):
                for ty in range(3):
                    both = jnp.concatenate([even[h][ty], odd[h][ty]], 0).astype(BF16)
                    stack[ty, x + 1, h, pl.ds(pl.multiple_of(pair * 16, 16), 16)] = both
        return carry

    lax.fori_loop(0, BRICKS // 2, gather, 0)

    bias_row = jnp.concatenate([bias[...]] * 4, 1)
    sends = []
    for h in range(2):
        total = None
        for ty in range(3):
            window = jnp.concatenate(
                [stack[ty, tx : tx + 8, h].reshape(ROWS, BAND) for tx in range(3)], 1
            )
            part = jnp.dot(window, band[ty], preferred_element_type=F32)
            if ty != 1:
                part = pltpu.roll(part.reshape(64, 8, HALF), 1 if ty == 0 else 7, 1)
                part = part.reshape(ROWS, HALF)
            total = part if total is None else total + part
        v = total + bias_row
        own = stack[1, 1:9, h, :, 0:HALF].reshape(ROWS, HALF).astype(F32)
        act = 0.5 * v * (1.0 + jnp.tanh(0.5 * v))
        hidden[...] = (own + act).astype(BF16).reshape(4, 2, 64, HALF)
        coarse = jnp.dot(
            hidden[:, 0].reshape(256, HALF), dband[0], preferred_element_type=F32
        ) + jnp.dot(hidden[:, 1].reshape(256, HALF), dband[1], preferred_element_type=F32)
        odd_rows = pltpu.roll(coarse[:, 256:].reshape(32, 8, 256), 7, 1).reshape(256, 256)
        coarse = (coarse[:, :256] + odd_rows).astype(BF16)
        placed = jnp.dot(place[...], coarse, preferred_element_type=F32).astype(BF16)
        lanes = pl.ds(h * 256, 256)
        stage[:, :, h * 256 : (h + 1) * 256] = placed.reshape(2 * size_y, 16, 256)
        for d in range(1, size_y):
            dest = lax.rem(j + d, size_y)
            copy = pltpu.make_async_remote_copy(
                src_ref=stage.at[pl.ds(dest * 2, 2), :, lanes],
                dst_ref=out_ref.at[pl.ds(j * 2, 2), :, lanes],
                send_sem=out_send.at[h, d],
                recv_sem=out_recv.at[h, d],
                device_id=(i, dest),
                device_id_type=MESH,
            )
            copy.start()
            sends.append(copy)
        copy = pltpu.make_async_copy(
            stage.at[pl.ds(j * 2, 2), :, lanes], out_ref.at[pl.ds(j * 2, 2), :, lanes], own_sem.at[h]
        )
        copy.start()
        sends.append(copy)
    for copy in sends:
        copy.wait()


def shards(features, neighbour_ids, conv_weight, conv_bias, down_weight, coarse_owner):
    size_x = lax.axis_size("bx")
    size_y = lax.axis_size("by")
    slots = 2 * size_y
    any_spec = pl.BlockSpec(memory_space=pl.ANY)
    out = pl.pallas_call(
        functools.partial(kernel, size_x, size_y),
        out_shape=jax.ShapeDtypeStruct((slots, 16, 4 * CO), BF16),
        in_specs=[any_spec] * 6,
        out_specs=any_spec,
        scratch_shapes=[
            pltpu.SMEM((BRICKS, 27), jnp.int32),
            pltpu.SMEM((BRICKS, 1), jnp.int32),
            pltpu.VMEM((ROWS, LANES), BF16),
            pltpu.VMEM((27, CH, CH), BF16),
            pltpu.VMEM((1, CH), F32),
            pltpu.VMEM((8, CH, CO), BF16),
            pltpu.SMEM((BRICKS, 27), jnp.int32),
            pltpu.VMEM((4, MESSAGE, LANES), BF16),
            pltpu.VMEM((4, MESSAGE, LANES), BF16),
            pltpu.VMEM((4, 16, LANES), BF16),
            pltpu.VMEM((T_SIZE, EDGE, LANES), F32),
            pltpu.VMEM((2, Y_SIZE, EDGE, LANES), F32),
            pltpu.VMEM((4, E_SIZE, EDGE, LANES), F32),
            pltpu.VMEM((3, 10, 2, FACE, BAND), BF16),
            pltpu.VMEM((3, 3 * BAND, HALF), BF16),
            pltpu.VMEM((2, HALF, 512), BF16),
            pltpu.VMEM((16 * slots, 256), BF16),
            pltpu.VMEM((4, 2, FACE, HALF), BF16),
            pltpu.VMEM((slots, 16, 4 * CO), BF16),
            pltpu.SemaphoreType.DMA((6,)),
            pltpu.SemaphoreType.DMA((8,)),
            pltpu.SemaphoreType.DMA((8,)),
            pltpu.SemaphoreType.DMA((2, 16)),
            pltpu.SemaphoreType.DMA((2, 16)),
            pltpu.SemaphoreType.DMA((2,)),
        ],
        compiler_params=pltpu.CompilerParams(
            collective_id=0, has_side_effects=True, vmem_limit_bytes=48 * 1024 * 1024
        ),
        name="brick_encoder",
    )(
        neighbour_ids,
        coarse_owner,
        features.reshape(ROWS, LANES),
        conv_weight,
        conv_bias.reshape(1, CH),
        down_weight,
    )
    return out.reshape(slots, 4, 4, 4 * CO)


def solution(mesh):
    in_specs = (
        P(("bx", "by"), None, None, None),
        P(("bx", "by"), None),
        P(),
        P(),
        P(),
        P(("bx", "by"), None),
    )
    out_specs = P(("bx", "by"), None, None, None)
    return jax.shard_map(shards, mesh=mesh, in_specs=in_specs, out_specs=out_specs, check_vma=False)
```

```python
import functools

import jax
import jax.numpy as jnp
from jax import lax
from jax.experimental import pallas as pl
from jax.experimental.pallas import tpu as pltpu
from jax.sharding import PartitionSpec as P

MESH = pl.DeviceIdType.MESH
F32 = jnp.float32
BF16 = jnp.bfloat16

EDGE = 8
BRICKS = 8
CH = 64
CO = 128
LANES = EDGE * CH
ROWS = BRICKS * EDGE * EDGE
HALF = 4 * CH
BAND = 6 * CH
FACE = BRICKS * EDGE
MESSAGE = FACE + 2 * BRICKS

T_FACE = BRICKS * EDGE
T_ZERO = T_FACE + 2 * BRICKS
T_SIZE = T_ZERO + EDGE
Y_ZERO = 2 * BRICKS
Y_SIZE = Y_ZERO + 1
E_ZERO = 4 * BRICKS
E_SIZE = E_ZERO + 1

STEPS = (-1, 0, 1)
SIDE = 4
HALO = [(1, 0), (-1, 0), (0, 1), (0, -1), (1, 1), (1, -1), (-1, 1), (-1, -1)]


def iota(shape, dim):
    return lax.broadcasted_iota(jnp.int32, shape, dim)


def picked_rows(message):
    inner = iota((MESSAGE, 128), 0)
    lane = iota((MESSAGE, 128), 1)
    brick, other = inner >> 3, inner & 7
    second = inner >= FACE + BRICKS
    if message < 2:
        at = 56 if message == 0 else 0
        face = brick * 64 + at + other
        edge = other * 64 + at + jnp.where(second, 0, 7)
    else:
        at = 7 if message == 2 else 0
        face = inner * 8 + at
        edge = other * 64 + at + jnp.where(second, 0, 56)
    target = jnp.where(inner < FACE, face, edge) - lane
    blocks = [(target == 128 * k).astype(F32) for k in range(ROWS // 128)]
    return jnp.concatenate(blocks, 1).astype(BF16)


def repeat_rows(target, corner, first, rows):
    for k in range(BRICKS):
        target[corner, first + k] = jnp.broadcast_to(rows[k : k + 1], (EDGE, LANES))


def kernel(
    size_x, size_y,
    ids_hbm, owner_hbm, feat_hbm, conv_hbm, bias_hbm, down_hbm,
    out_ref,
    ids, owner, feat, conv, bias, down,
    index, sendbuf, xy_recv, edge_recv, table, ytab, etab,
    stack, band, dband, named, place, raw, relay, ready,
    load_sem, halo_send, halo_recv, name_send, name_recv,
    raw_send, raw_recv, out_send, out_recv, own_sem,
):
    i = lax.axis_index("bx")
    j = lax.axis_index("by")
    z, y = j // SIDE, j % SIDE

    loads = [
        pltpu.make_async_copy(source, target, load_sem.at[k])
        for k, (source, target) in enumerate(
            [
                (feat_hbm, feat),
                (conv_hbm, conv),
                (ids_hbm, ids),
                (owner_hbm, owner),
                (bias_hbm, bias),
                (down_hbm, down),
            ]
        )
    ]
    for load in loads:
        load.start()

    def beside(step_x, step_y):
        return (lax.rem(i + step_x + size_x, size_x), lax.rem(j + step_y + size_y, size_y))

    def partner(h, d):
        if h == 0:
            return (i, z * SIDE + lax.rem(y + d, SIDE))
        return (i, lax.rem(z + d, SIDE) * SIDE + y)

    barrier = pltpu.get_barrier_semaphore()
    greeted = [beside(sx, sy) for sx, sy in HALO]
    greeted += [partner(h, d) for h in range(2) for d in range(1, SIDE)]
    for device in greeted:
        pl.semaphore_signal(barrier, inc=1, device_id=device, device_id_type=MESH)

    def remote(source, target, send_sem, recv_sem, device):
        copy = pltpu.make_async_remote_copy(
            src_ref=source,
            dst_ref=target,
            send_sem=send_sem,
            recv_sem=recv_sem,
            device_id=device,
            device_id_type=MESH,
        )
        copy.start()
        return copy

    picks = [picked_rows(k) for k in range(4)]
    loads[0].wait()
    picked = []
    for k in range(4):
        picked.append(jnp.dot(picks[k], feat[...], preferred_element_type=F32))
        sendbuf[k] = picked[k].astype(BF16)

    pl.semaphore_wait(barrier, len(greeted))
    copies = []
    for k, (sx, sy) in enumerate(HALO):
        if k < 4:
            source, target = sendbuf.at[k], xy_recv.at[k]
        else:
            source = sendbuf.at[(k - 4) // 2, pl.ds(FACE, 16)]
            target = edge_recv.at[k - 4]
        copies.append(
            remote(source, target, halo_send.at[k], halo_recv.at[k], beside(sx, sy))
        )

    loads[3].wait()
    owners = [owner[0, g] for g in range(BRICKS)]
    lane = iota((EDGE, 128), 1)
    slot_of = jnp.zeros((EDGE, 128), jnp.int32)
    for g in range(BRICKS):
        rank = jnp.int32(0)
        for earlier in range(g):
            rank = rank + jnp.where(owners[earlier] == owners[g], 1, 0)
        slot_of = jnp.where(lane // 16 == g, owners[g] * 2 + rank, slot_of)
    named[0, 0] = slot_of.astype(F32)
    name_copies = [
        remote(named.at[0, 0], named.at[h, d], name_send.at[h, d], name_recv.at[h, d], partner(h, d))
        for h in range(2)
        for d in range(1, SIDE)
    ]

    table[0:T_FACE] = feat[...].astype(F32).reshape(T_FACE, EDGE, LANES)
    table[T_ZERO:T_SIZE] = jnp.zeros((EDGE, EDGE, LANES), F32)
    for k in range(2):
        ytab[k, 0:BRICKS] = picked[2 + k][0:FACE].reshape(BRICKS, EDGE, LANES)
        ytab[k, Y_ZERO] = jnp.zeros((EDGE, LANES), F32)
    for k in range(4):
        first = FACE + k % 2 * BRICKS
        repeat_rows(etab, k, 0, picked[k // 2][first : first + BRICKS])
        etab[k, E_ZERO] = jnp.zeros((EDGE, LANES), F32)

    loads[2].wait()
    for g in range(BRICKS):
        for tap in range(27):
            sx, sy = tap // 9 - 1, tap // 3 % 3 - 1
            value = ids[g, tap]
            brick = value & 7
            far_x = jnp.where(value >> 3 >> 4 == i, 0, 1)
            far_y = jnp.where((value >> 3) & 15 == j, 0, 1)
            if sx == 0 and sy == 0:
                row, zero = brick * EDGE, T_ZERO
            elif sy == 0:
                edge_x, side = (7, 0) if sx < 0 else (0, 1)
                row = jnp.where(far_x == 0, brick * EDGE + edge_x, T_FACE + side * BRICKS + brick)
                zero = T_ZERO
            elif sx == 0:
                row, zero = far_y * BRICKS + brick, Y_ZERO
            else:
                row, zero = far_x * 16 + far_y * 8 + brick, E_ZERO
            index[g, tap] = jnp.where(value >= 0, row, zero)

    loads[1].wait()
    empty = jnp.zeros((CH, CH), BF16)
    blank = jnp.zeros((CH, 2 * CH), BF16)
    for ty in range(3):
        for tx in range(3):
            w = [conv[tx * 9 + ty * 3 + tz] * jnp.array(0.5, BF16) for tz in range(3)]
            pairs = {
                -1: jnp.concatenate([w[0], empty], 1),
                0: jnp.concatenate([w[1], w[0]], 1),
                1: jnp.concatenate([w[2], w[1]], 1),
                2: jnp.concatenate([empty, w[2]], 1),
            }
            for place_in, depth_in in enumerate((0, 1, 2, 3, 4, -1)):
                for q in range(2):
                    first = tx * BAND + place_in * CH
                    band[ty, first : first + CH, q * 128 : (q + 1) * 128] = pairs.get(
                        depth_in - 2 * q, blank
                    )
    loads[5].wait()
    for a in range(2):
        for k in range(4):
            for b in range(2):
                for half in range(2):
                    first = b * 256 + half * 128
                    block = down[a * 4 + b * 2 + k % 2] if k // 2 == half else blank
                    dband[a * HALF + k * CH : a * HALF + (k + 1) * CH, first : first + 128] = block

    for copy in name_copies:
        copy.wait()
    same_xy = iota((16, 128), 0) == (iota((16, 128), 1) & 15)
    for h in range(2):
        for d in range(SIDE):
            slots = named[h, d] if d else named[0, 0]
            slots = jnp.where(same_xy, jnp.concatenate([slots, slots], 0), -1.0)
            for far in range(SIDE):
                device = far * SIDE + y if h == 0 else z * SIDE + far
                for rank in range(2):
                    wanted = (device * 2 + rank).astype(F32)
                    first = (far * 2 + rank) * 16
                    place[h, d, first : first + 16] = (slots == wanted).astype(F32).astype(BF16)

    loads[4].wait()
    for copy in copies:
        copy.wait()
    for k in range(2):
        over_x = xy_recv[k].astype(F32)
        over_y = xy_recv[2 + k].astype(F32)
        first = T_FACE + k * BRICKS
        table[first : first + BRICKS] = over_x[0:FACE].reshape(BRICKS, EDGE, LANES)
        ytab[k, BRICKS : 2 * BRICKS] = over_y[0:FACE].reshape(BRICKS, EDGE, LANES)
        for side in range(2):
            first = FACE + side * BRICKS
            repeat_rows(etab, side * 2 + k, 8, over_y[first : first + BRICKS])
            repeat_rows(etab, k * 2 + side, 16, over_x[first : first + BRICKS])
            diagonal = edge_recv[k * 2 + side].astype(F32)
            diagonal = diagonal[side * BRICKS : (side + 1) * BRICKS]
            repeat_rows(etab, k * 2 + side, 24, diagonal)

    low = iota((EDGE, 128), 1) < CH
    last_row = iota((EDGE, BAND), 0) == 7
    first_row = iota((EDGE, BAND), 0) == 0

    def halves(read, centre, minus, plus):
        c = read(centre, 0, LANES)
        m = read(minus, LANES - 128, LANES)
        p = read(plus, 0, 128)
        e0 = jnp.where(low, c[:, 256:384], m)
        e1 = jnp.where(low, p, c[:, 128:256])
        return (
            jnp.concatenate([c[:, 0:256], e0], 1),
            jnp.concatenate([c[:, 256:512], e1], 1),
        )

    def one_slab(g, x):
        sx = -1 if x < 0 else (1 if x > 7 else 0)
        shift = x if sx == 0 else 0
        result = []
        for sy in STEPS:
            tap = (sx + 1) * 9 + (sy + 1) * 3
            if sy == 0:
                def read(row, low_lane, high_lane):
                    return table[row + shift, :, low_lane:high_lane]
            elif sx == 0:
                def read(row, low_lane, high_lane, side=(sy + 1) // 2):
                    lines = ytab[side, row, :, low_lane:high_lane]
                    return pltpu.roll(lines, (7 - x if side == 0 else 0 - x) & 7, 0)
            else:
                def read(row, low_lane, high_lane, corner=(sx + 1) // 2 * 2 + (sy + 1) // 2):
                    return etab[corner, row, :, low_lane:high_lane]
            result.append(halves(read, index[g, tap + 1], index[g, tap], index[g, tap + 2]))
        before, same, after = result
        return [
            [jnp.where(last_row, before[h], same[h]), same[h], jnp.where(first_row, after[h], same[h])]
            for h in range(2)
        ]

    def gather(pair, slabs):
        for x in slabs:
            even = one_slab(pair * 2, x)
            odd = one_slab(pair * 2 + 1, x)
            for h in range(2):
                for ty in range(3):
                    both = jnp.concatenate([even[h][ty], odd[h][ty]], 0)
                    stack[pair, ty, x + 1, h] = both.astype(BF16)

    bias_row = jnp.concatenate([bias[...] * 0.5] * 4, 1)
    row, col = iota((32, 64), 0), iota((32, 64), 1)
    even_rows = ((row & 15) >> 2) * 16 + (row >> 4) * 8 + (row & 3) * 2 == col
    even_rows = even_rows.astype(F32).astype(BF16)
    pairs = BRICKS // 2
    parts = [range(-1, 3), range(3, 6), range(6, 9)]
    raw_copies = []
    gather(0, range(-1, 9))
    for pair in range(pairs):
        total = None
        for ty in range(3):
            window = jnp.concatenate(
                [stack[pair, ty, tx : tx + 8].reshape(256, BAND) for tx in range(3)], 1
            )
            part = jnp.dot(window, band[ty], preferred_element_type=F32)
            if ty != 1:
                part = pltpu.roll(part.reshape(32, 8, HALF), 1 if ty == 0 else 7, 1)
                part = part.reshape(256, HALF)
            total = part if total is None else total + part
            if pair + 1 < pairs:
                gather(pair + 1, parts[ty])
        half_v = total + bias_row
        own = stack[pair, 1, 1:9, :, :, 0:HALF].reshape(256, HALF).astype(F32)
        hidden = (own + (half_v + half_v * jnp.tanh(half_v))).astype(BF16)
        hidden = hidden.reshape(4, 2, 32, HALF)
        hidden = jnp.concatenate(
            [hidden[:, 0].reshape(128, HALF), hidden[:, 1].reshape(128, HALF)], 1
        )
        coarse = jnp.dot(hidden, dband[...], preferred_element_type=F32)
        odd = pltpu.roll(coarse[:, 256:].reshape(16, 8, 256), 7, 1).reshape(128, 256)
        coarse = (coarse[:, :256] + odd).astype(BF16).reshape(4, 2, 16, 256)
        for h in range(2):
            piece = jnp.dot(
                even_rows, coarse[:, h].reshape(64, 256), preferred_element_type=F32
            )
            raw[h, pair * 2 : pair * 2 + 2] = piece.astype(BF16).reshape(2, 16, 256)
        if pair % 2 == 1:
            some = pl.ds(pair * 2 - 2, 4)
            for h in range(2):
                for d in range(1, SIDE):
                    raw_copies.append(
                        remote(
                            raw.at[h, some],
                            relay.at[h, d, some],
                            raw_send.at[h, pair // 2, d],
                            raw_recv.at[h, pair // 2, d],
                            partner(h, d),
                        )
                    )

    def forward(h, d):
        pieces = raw[h] if d == 0 else relay[h, d]
        placed = jnp.dot(
            place[h, d], pieces.reshape(128, 256), preferred_element_type=F32
        ).astype(BF16)
        source = lax.rem((y if h == 0 else z) - d + SIDE, SIDE)
        ready[h, :, source] = placed.reshape(SIDE, 2, 16, 256)

    for h in range(2):
        forward(h, 0)
    for copy in raw_copies:
        copy.wait()
    out_copies = []
    for h in range(2):
        for d in range(1, SIDE):
            forward(h, d)
        lanes = pl.ds(h * 256, 256)
        target = out_ref.at[z, :, :, :, lanes] if h == 0 else out_ref.at[:, y, :, :, lanes]
        here = z if h == 0 else y
        for d in range(1, SIDE):
            out_copies.append(
                remote(
                    ready.at[h, lax.rem(here + d, SIDE)],
                    target,
                    out_send.at[h, d],
                    out_recv.at[h, d],
                    partner(1 - h, d),
                )
            )
        copy = pltpu.make_async_copy(ready.at[h, here], target, own_sem.at[h])
        copy.start()
        out_copies.append(copy)
    for copy in out_copies:
        copy.wait()


def shards(features, neighbour_ids, conv_weight, conv_bias, down_weight, coarse_owner):
    size_x = lax.axis_size("bx")
    size_y = lax.axis_size("by")
    slots = 2 * size_y
    hbm_spec = pl.BlockSpec(memory_space=pltpu.HBM)
    out = pl.pallas_call(
        functools.partial(kernel, size_x, size_y),
        out_shape=jax.ShapeDtypeStruct((SIDE, SIDE, 2, 16, 4 * CO), BF16),
        in_specs=[hbm_spec] * 6,
        out_specs=pl.BlockSpec(memory_space=pl.ANY),
        scratch_shapes=[
            pltpu.SMEM((BRICKS, 27), jnp.int32),
            pltpu.SMEM((1, BRICKS), jnp.int32),
            pltpu.VMEM((ROWS, LANES), BF16),
            pltpu.VMEM((27, CH, CH), BF16),
            pltpu.VMEM((1, CH), F32),
            pltpu.VMEM((8, CH, CO), BF16),
            pltpu.SMEM((BRICKS, 27), jnp.int32),
            pltpu.VMEM((4, MESSAGE, LANES), BF16),
            pltpu.VMEM((4, MESSAGE, LANES), BF16),
            pltpu.VMEM((4, 16, LANES), BF16),
            pltpu.VMEM((T_SIZE, EDGE, LANES), F32),
            pltpu.VMEM((2, Y_SIZE, EDGE, LANES), F32),
            pltpu.VMEM((4, E_SIZE, EDGE, LANES), F32),
            pltpu.VMEM((BRICKS // 2, 3, 10, 2, 16, BAND), BF16),
            pltpu.VMEM((3, 3 * BAND, HALF), BF16),
            pltpu.VMEM((2 * HALF, 512), BF16),
            pltpu.VMEM((2, SIDE, EDGE, 128), F32),
            pltpu.VMEM((2, SIDE, 128, 128), BF16),
            pltpu.VMEM((2, BRICKS, 16, 256), BF16),
            pltpu.VMEM((2, SIDE, BRICKS, 16, 256), BF16),
            pltpu.VMEM((2, SIDE, SIDE, 2, 16, 256), BF16),
            pltpu.SemaphoreType.DMA((6,)),
            pltpu.SemaphoreType.DMA((8,)),
            pltpu.SemaphoreType.DMA((8,)),
            pltpu.SemaphoreType.DMA((2, SIDE)),
            pltpu.SemaphoreType.DMA((2, SIDE)),
            pltpu.SemaphoreType.DMA((2, 2, SIDE)),
            pltpu.SemaphoreType.DMA((2, 2, SIDE)),
            pltpu.SemaphoreType.DMA((2, SIDE)),
            pltpu.SemaphoreType.DMA((2, SIDE)),
            pltpu.SemaphoreType.DMA((2,)),
        ],
        compiler_params=pltpu.CompilerParams(
            collective_id=0, has_side_effects=True, vmem_limit_bytes=48 * 1024 * 1024
        ),
        name="brick_encoder",
    )(
        neighbour_ids,
        coarse_owner.reshape(1, BRICKS),
        features.reshape(ROWS, LANES),
        conv_weight,
        conv_bias.reshape(1, CH),
        down_weight,
    )
    return out.reshape(slots, 4, 4, 4 * CO)


def solution(mesh):
    in_specs = (
        P(("bx", "by"), None, None, None),
        P(("bx", "by"), None),
        P(),
        P(),
        P(),
        P(("bx", "by"), None),
    )
    out_specs = P(("bx", "by"), None, None, None)
    return jax.shard_map(shards, mesh=mesh, in_specs=in_specs, out_specs=out_specs, check_vma=False)
```

```python
import functools

import jax
import jax.numpy as jnp
from jax import lax
from jax.experimental import pallas as pl
from jax.experimental.pallas import tpu as pltpu
from jax.sharding import PartitionSpec as P

MESH = pl.DeviceIdType.MESH
F32 = jnp.float32
BF16 = jnp.bfloat16

EDGE = 8
BRICKS = 8
CH = 64
CO = 128
LANES = EDGE * CH
ROWS = BRICKS * EDGE * EDGE
HALF = 4 * CH
BAND = 6 * CH
FACE = BRICKS * EDGE

T_FACE = BRICKS * EDGE
T_ZERO = T_FACE + 2 * BRICKS
T_SIZE = T_ZERO + EDGE
Y_ZERO = 2 * BRICKS
Y_SIZE = Y_ZERO + 1
E_ZERO = 4 * BRICKS
E_SIZE = E_ZERO + 1

STEPS = (-1, 0, 1)
CHUNK = 1
CHUNKS = EDGE // 2 // CHUNK
SENT = 8 * CHUNK
HALO = [(1, 0), (-1, 0), (0, 1), (0, -1), (1, 1), (1, -1), (-1, 1), (-1, -1)]


def iota(shape, dim):
    return lax.broadcasted_iota(jnp.int32, shape, dim)


def picked_rows():
    targets = []
    inner = iota((FACE, 128), 0)
    for first in (56, 0):
        targets.append((inner >> 3) * 64 + first + (inner & 7))
    for first in (7, 0):
        targets.append(inner * 8 + first)
    inner = iota((4 * BRICKS, 128), 0)
    corner = inner >> 3
    targets.append(
        (inner & 7) * 64 + jnp.where(corner < 2, 56, 0) + jnp.where(corner & 1 == 0, 7, 0)
    )
    target = jnp.concatenate(targets, 0)
    target = target - iota(target.shape, 1)
    blocks = [(target == 128 * k).astype(F32) for k in range(ROWS // 128)]
    return jnp.concatenate(blocks, 1).astype(BF16)


def repeat_rows(target, corner, first, rows, start=0, step=1):
    for k in range(BRICKS):
        row = start + step * k
        target[corner, first + k] = jnp.broadcast_to(rows[row : row + 1], (EDGE, LANES))


def kernel(
    size_x, size_y,
    ids_hbm, owner_hbm, feat_hbm, conv_hbm, bias_hbm, down_hbm,
    out_ref,
    ids, owner, feat, conv, bias, down,
    index, face_send, edge_send, face_recv, edge_recv, table, ytab, etab,
    stack, band, down_both, place, stage,
    load_sem, halo_send, halo_recv, out_send, out_recv, own_sem,
):
    i = lax.axis_index("bx")
    j = lax.axis_index("by")

    loads = [
        pltpu.make_async_copy(source, target, load_sem.at[k])
        for k, (source, target) in enumerate(
            [
                (feat_hbm, feat),
                (conv_hbm, conv),
                (ids_hbm, ids),
                (owner_hbm, owner),
                (bias_hbm, bias),
                (down_hbm, down),
            ]
        )
    ]
    for load in loads:
        load.start()

    def beside(step_x, step_y):
        return (lax.rem(i + step_x + size_x, size_x), lax.rem(j + step_y + size_y, size_y))

    barrier = pltpu.get_barrier_semaphore()
    greeted = [beside(sx, sy) for sx, sy in HALO if sx]
    greeted += [beside(0, d) for d in range(1, size_y)]
    for device in greeted:
        pl.semaphore_signal(barrier, inc=1, device_id=device, device_id_type=MESH)

    def remote(source, target, send_sem, recv_sem, device):
        copy = pltpu.make_async_remote_copy(
            src_ref=source,
            dst_ref=target,
            send_sem=send_sem,
            recv_sem=recv_sem,
            device_id=device,
            device_id_type=MESH,
        )
        copy.start()
        return copy

    pick = picked_rows()
    loads[0].wait()
    picked = jnp.dot(pick, feat[...], preferred_element_type=F32)
    for k in range(4):
        face_send[k] = picked[k * FACE : (k + 1) * FACE].astype(BF16)
        first = 4 * FACE + k * BRICKS
        edge = picked[first : first + BRICKS]
        edge_send[k] = jnp.concatenate([edge[:, 0:256], edge[:, 256:512]], 0).astype(BF16)

    pl.semaphore_wait(barrier, len(greeted))
    copies = []
    for k, (sx, sy) in enumerate(HALO):
        if k < 4:
            source, target = face_send.at[k], face_recv.at[k]
        else:
            source, target = edge_send.at[k - 4], edge_recv.at[k - 4]
        copies.append(
            remote(source, target, halo_send.at[k], halo_recv.at[k], beside(sx, sy))
        )

    table[0:T_FACE] = feat[...].astype(F32).reshape(T_FACE, EDGE, LANES)
    table[T_ZERO:T_SIZE] = jnp.zeros((EDGE, EDGE, LANES), F32)
    for k in range(2):
        ytab[k, 0:BRICKS] = picked[(2 + k) * FACE : (3 + k) * FACE].reshape(BRICKS, EDGE, LANES)
        ytab[k, Y_ZERO] = jnp.zeros((EDGE, LANES), F32)
    for k in range(4):
        repeat_rows(etab, k, 0, picked, 4 * FACE + k * BRICKS)
        etab[k, E_ZERO] = jnp.zeros((EDGE, LANES), F32)

    loads[2].wait()
    for g in range(BRICKS):
        for tap in range(27):
            sx, sy = tap // 9 - 1, tap // 3 % 3 - 1
            value = ids[g, tap]
            brick = value & 7
            far_x = jnp.where(value >> 3 >> 4 == i, 0, 1)
            far_y = jnp.where((value >> 3) & 15 == j, 0, 1)
            if sx == 0 and sy == 0:
                row, zero = brick * EDGE, T_ZERO
            elif sy == 0:
                edge_x, side = (7, 0) if sx < 0 else (0, 1)
                row = jnp.where(far_x == 0, brick * EDGE + edge_x, T_FACE + side * BRICKS + brick)
                zero = T_ZERO
            elif sx == 0:
                row, zero = far_y * BRICKS + brick, Y_ZERO
            else:
                row, zero = far_x * 16 + far_y * 8 + brick, E_ZERO
            index[g, tap] = jnp.where(value >= 0, row, zero)

    loads[1].wait()
    empty = jnp.zeros((CH, CH), BF16)
    blank = jnp.zeros((CH, 2 * CH), BF16)
    for ty in range(3):
        for tx in range(3):
            w = [conv[tx * 9 + ty * 3 + tz] * jnp.array(0.5, BF16) for tz in range(3)]
            pairs = {
                -1: jnp.concatenate([w[0], empty], 1),
                0: jnp.concatenate([w[1], w[0]], 1),
                1: jnp.concatenate([w[2], w[1]], 1),
                2: jnp.concatenate([empty, w[2]], 1),
            }
            for place_in, depth_in in enumerate((0, 1, 2, 3, 4, -1)):
                for q in range(2):
                    first = tx * BAND + place_in * CH
                    band[ty, first : first + CH, q * 128 : (q + 1) * 128] = pairs.get(
                        depth_in - 2 * q, blank
                    )
    loads[5].wait()
    for a in range(2):
        for b in range(2):
            for k in range(2):
                first = (a * 2 + k) * CH
                down_both[first : first + CH, b * CO : (b + 1) * CO] = down[a * 4 + b * 2 + k]

    loads[3].wait()
    owners = [owner[0, g] for g in range(BRICKS)]
    row, col = iota((4 * CHUNK, 64 * CHUNK), 0), iota((4 * CHUNK, 64 * CHUNK), 1)
    slot_of = jnp.zeros((4 * CHUNK, 64 * CHUNK), jnp.int32)
    for g in range(BRICKS):
        rank = jnp.int32(0)
        for earlier in range(g):
            rank = rank + jnp.where(owners[earlier] == owners[g], 1, 0)
        slot_of = jnp.where((col >> 3) & 7 == g, owners[g] * 2 + rank, slot_of)
    slot_of = jnp.where((col >> 6 == row >> 2) & (col & 7 == (row & 3) * 2), slot_of, -1)
    rows = 8 if CHUNK == 1 else 4 * CHUNK
    slot_of = jnp.concatenate([slot_of] * (rows // (4 * CHUNK)), 0)
    row = iota(slot_of.shape, 0) >> (2 + CHUNK - 1)
    for s in range(0, 2 * size_y, rows // (4 * CHUNK)):
        block = (slot_of == row + s).astype(F32) if CHUNK == 1 else (slot_of == s).astype(F32)
        first = s * 4 * CHUNK
        place[first : first + rows] = block

    loads[4].wait()
    for copy in copies:
        copy.wait()
    for k in range(2):
        over_x = face_recv[k].astype(F32)
        over_y = face_recv[2 + k].astype(F32)
        first = T_FACE + k * BRICKS
        table[first : first + BRICKS] = over_x.reshape(BRICKS, EDGE, LANES)
        ytab[k, BRICKS : 2 * BRICKS] = over_y.reshape(BRICKS, EDGE, LANES)
        for side in range(2):
            at = 0 if side else 7
            repeat_rows(etab, side * 2 + k, 8, over_y, at, EDGE)
            repeat_rows(etab, k * 2 + side, 16, over_x, at, EDGE)
            edge = edge_recv[k * 2 + side].astype(F32)
            edge = jnp.concatenate([edge[0:8], edge[8:16]], 1)
            repeat_rows(etab, k * 2 + side, 24, edge)

    low = iota((EDGE, 128), 1) < CH
    last_row = iota((EDGE, BAND), 0) == 7
    first_row = iota((EDGE, BAND), 0) == 0

    def halves(read, centre, minus, plus):
        c = read(centre, 0, LANES)
        m = read(minus, LANES - 128, LANES)
        p = read(plus, 0, 128)
        e0 = jnp.where(low, c[:, 256:384], m)
        e1 = jnp.where(low, p, c[:, 128:256])
        return (
            jnp.concatenate([c[:, 0:256], e0], 1),
            jnp.concatenate([c[:, 256:512], e1], 1),
        )

    def one_slab(g, x):
        sx = -1 if x < 0 else (1 if x > 7 else 0)
        shift = x if sx == 0 else 0
        result = []
        for sy in STEPS:
            tap = (sx + 1) * 9 + (sy + 1) * 3
            if sy == 0:
                def read(row, low_lane, high_lane):
                    return table[row + shift, :, low_lane:high_lane]
            elif sx == 0:
                def read(row, low_lane, high_lane, side=(sy + 1) // 2):
                    lines = ytab[side, row, :, low_lane:high_lane]
                    return pltpu.roll(lines, (7 - x if side == 0 else 0 - x) & 7, 0)
            else:
                def read(row, low_lane, high_lane, corner=(sx + 1) // 2 * 2 + (sy + 1) // 2):
                    return etab[corner, row, :, low_lane:high_lane]
            result.append(halves(read, index[g, tap + 1], index[g, tap], index[g, tap + 2]))
        before, same, after = result
        return [
            [jnp.where(last_row, before[h], same[h]), same[h], jnp.where(first_row, after[h], same[h])]
            for h in range(2)
        ]

    def gather(slabs):
        for x in slabs:
            for pair in range(BRICKS // 2):
                even = one_slab(pair * 2, x)
                odd = one_slab(pair * 2 + 1, x)
                for h in range(2):
                    for ty in range(3):
                        both = jnp.concatenate([even[h][ty], odd[h][ty]], 0)
                        stack[ty, x + 1, h, pair * 16 : pair * 16 + 16] = both.astype(BF16)

    def out_copy(chunk, d):
        dest = lax.rem(j + d, size_y)
        return pltpu.make_async_remote_copy(
            src_ref=stage.at[chunk, dest],
            dst_ref=out_ref.at[j, chunk],
            send_sem=out_send.at[chunk, d],
            recv_sem=out_recv.at[chunk, d],
            device_id=(i, dest),
            device_id_type=MESH,
        )

    def own_copy(chunk):
        return pltpu.make_async_copy(stage.at[chunk, j], out_ref.at[j, chunk], own_sem.at[chunk])

    bias_row = jnp.concatenate([bias[...] * 0.5] * 4, 1)
    slabs = 2 * CHUNK
    size = slabs * 2 * FACE
    gather([-1, 0])
    for chunk in range(CHUNKS):
        base = chunk * slabs
        gather(range(base + 1, base + slabs + 1))
        total = None
        for ty in range(3):
            window = jnp.concatenate(
                [
                    stack[ty, base + tx : base + tx + slabs].reshape(size, BAND)
                    for tx in range(3)
                ],
                1,
            )
            part = jnp.dot(window, band[ty], preferred_element_type=F32)
            if ty != 1:
                part = pltpu.roll(part.reshape(size // 8, 8, HALF), 1 if ty == 0 else 7, 1)
                part = part.reshape(size, HALF)
            total = part if total is None else total + part
        half_v = total + bias_row
        own = stack[1, base + 1 : base + 1 + slabs, :, :, 0:HALF].reshape(size, HALF)
        hidden = own.astype(F32) + (half_v + half_v * jnp.tanh(half_v))
        hidden = hidden.astype(BF16).reshape(CHUNK, 2, 2 * FACE, HALF)
        lhs = jnp.concatenate(
            [
                jnp.concatenate([hidden[:, a, :, k * 128 : (k + 1) * 128] for a in range(2)], 2)
                for k in range(2)
            ],
            0,
        ).reshape(2 * CHUNK * 2 * FACE, 256)
        coarse = jnp.dot(lhs, down_both[...], preferred_element_type=F32)
        odd = pltpu.roll(coarse[:, CO:].reshape(-1, 8, CO), 7, 1).reshape(-1, CO)
        coarse = (coarse[:, :CO] + odd).astype(BF16).reshape(2, CHUNK, 2, FACE, CO)
        coarse = jnp.concatenate(
            [coarse[k, :, h] for h in range(2) for k in range(2)], 2
        ).reshape(CHUNK * FACE, 4 * CO)
        placed = jnp.dot(place[...].astype(BF16), coarse, preferred_element_type=F32)
        stage[chunk] = placed.reshape(size_y, SENT, 4 * CO).astype(BF16)
        for d in range(1, size_y):
            out_copy(chunk, d).start()
        own_copy(chunk).start()
    for chunk in range(CHUNKS):
        for d in range(1, size_y):
            out_copy(chunk, d).wait()
        own_copy(chunk).wait()


def shards(features, neighbour_ids, conv_weight, conv_bias, down_weight, coarse_owner):
    size_x = lax.axis_size("bx")
    size_y = lax.axis_size("by")
    slots = 2 * size_y
    hbm_spec = pl.BlockSpec(memory_space=pltpu.HBM)
    out = pl.pallas_call(
        functools.partial(kernel, size_x, size_y),
        out_shape=jax.ShapeDtypeStruct((size_y, CHUNKS, SENT, 4 * CO), BF16),
        in_specs=[hbm_spec] * 6,
        out_specs=pl.BlockSpec(memory_space=pl.ANY),
        scratch_shapes=[
            pltpu.SMEM((BRICKS, 27), jnp.int32),
            pltpu.SMEM((1, BRICKS), jnp.int32),
            pltpu.VMEM((ROWS, LANES), BF16),
            pltpu.VMEM((27, CH, CH), BF16),
            pltpu.VMEM((1, CH), F32),
            pltpu.VMEM((8, CH, CO), BF16),
            pltpu.SMEM((BRICKS, 27), jnp.int32),
            pltpu.VMEM((4, FACE, LANES), BF16),
            pltpu.VMEM((4, 16, 256), BF16),
            pltpu.VMEM((4, FACE, LANES), BF16),
            pltpu.VMEM((4, 16, 256), BF16),
            pltpu.VMEM((T_SIZE, EDGE, LANES), F32),
            pltpu.VMEM((2, Y_SIZE, EDGE, LANES), F32),
            pltpu.VMEM((4, E_SIZE, EDGE, LANES), F32),
            pltpu.VMEM((3, 10, 2, FACE, BAND), BF16),
            pltpu.VMEM((3, 3 * BAND, HALF), BF16),
            pltpu.VMEM((256, 2 * CO), BF16),
            pltpu.VMEM((slots * 4 * CHUNK, FACE * CHUNK), F32),
            pltpu.VMEM((CHUNKS, size_y, SENT, 4 * CO), BF16),
            pltpu.SemaphoreType.DMA((6,)),
            pltpu.SemaphoreType.DMA((8,)),
            pltpu.SemaphoreType.DMA((8,)),
            pltpu.SemaphoreType.DMA((CHUNKS, size_y)),
            pltpu.SemaphoreType.DMA((CHUNKS, size_y)),
            pltpu.SemaphoreType.DMA((CHUNKS,)),
        ],
        compiler_params=pltpu.CompilerParams(
            collective_id=0, has_side_effects=True, vmem_limit_bytes=63 * 1024 * 1024
        ),
        name="brick_encoder",
    )(
        neighbour_ids,
        coarse_owner.reshape(1, BRICKS),
        features.reshape(ROWS, LANES),
        conv_weight,
        conv_bias.reshape(1, CH),
        down_weight,
    )
    out = out.reshape(size_y, CHUNKS, 2, CHUNK, 4, 4 * CO)
    return out.transpose(0, 2, 1, 3, 4, 5).reshape(slots, 4, 4, 4 * CO)


def solution(mesh):
    in_specs = (
        P(("bx", "by"), None, None, None),
        P(("bx", "by"), None),
        P(),
        P(),
        P(),
        P(("bx", "by"), None),
    )
    out_specs = P(("bx", "by"), None, None, None)
    return jax.shard_map(shards, mesh=mesh, in_specs=in_specs, out_specs=out_specs, check_vma=False)
```

```python
import functools

import jax
import jax.numpy as jnp
from jax import lax
from jax.experimental import pallas as pl
from jax.experimental.pallas import tpu as pltpu
from jax.sharding import PartitionSpec as P

MESH = pl.DeviceIdType.MESH
F32 = jnp.float32
BF16 = jnp.bfloat16

EDGE = 8
BRICKS = 8
CH = 64
CO = 128
LANES = EDGE * CH
ROWS = BRICKS * EDGE * EDGE
HALF = 4 * CH
BAND = 6 * CH
FACE = BRICKS * EDGE

T_FACE = BRICKS * EDGE
T_ZERO = T_FACE + 2 * BRICKS
T_SIZE = T_ZERO + EDGE
Y_ZERO = 2 * BRICKS
Y_SIZE = Y_ZERO + 1
E_ZERO = 4 * BRICKS
E_SIZE = E_ZERO + 1

STEPS = (-1, 0, 1)
CHUNK = 2
CHUNKS = EDGE // 2 // CHUNK
SIDE = 4
HALO = [(1, 0), (-1, 0), (0, 1), (0, -1), (1, 1), (1, -1), (-1, 1), (-1, -1)]


def iota(shape, dim):
    return lax.broadcasted_iota(jnp.int32, shape, dim)


def picked_rows():
    targets = []
    inner = iota((FACE, 128), 0)
    for first in (56, 0):
        targets.append((inner >> 3) * 64 + first + (inner & 7))
    for first in (7, 0):
        targets.append(inner * 8 + first)
    inner = iota((4 * BRICKS, 128), 0)
    corner = inner >> 3
    targets.append(
        (inner & 7) * 64 + jnp.where(corner < 2, 56, 0) + jnp.where(corner & 1 == 0, 7, 0)
    )
    target = jnp.concatenate(targets, 0)
    target = target - iota(target.shape, 1)
    blocks = [(target == 128 * k).astype(F32) for k in range(ROWS // 128)]
    return jnp.concatenate(blocks, 1).astype(BF16)


def repeat_rows(target, corner, first, rows, start=0, step=1):
    for k in range(BRICKS):
        row = start + step * k
        target[corner, first + k] = jnp.broadcast_to(rows[row : row + 1], (EDGE, LANES))


def kernel(
    size_x, size_y,
    ids_hbm, owner_hbm, feat_hbm, conv_hbm, bias_hbm, down_hbm,
    out_ref,
    ids, owner, feat, conv, bias, down,
    index, face_send, edge_send, face_recv, edge_recv, table, ytab, etab,
    stack, band, down_both, place, stage,
    load_sem, halo_send, halo_recv, out_send, out_recv, own_sem, known_sem,
):
    i = lax.axis_index("bx")
    j = lax.axis_index("by")
    z, y = j // SIDE, lax.rem(j, SIDE)

    loads = [
        pltpu.make_async_copy(source, target, load_sem.at[k])
        for k, (source, target) in enumerate(
            [
                (feat_hbm, feat),
                (conv_hbm, conv),
                (ids_hbm, ids),
                (owner_hbm, owner),
                (bias_hbm, bias),
                (down_hbm, down),
            ]
        )
    ]
    for load in loads:
        load.start()

    def inside(step_x, step_y):
        x_in = (i + step_x >= 0) & (i + step_x < size_x)
        return x_in & (j + step_y >= 0) & (j + step_y < size_y)

    def partner(step_z, step_y):
        return lax.rem(z + step_z, SIDE) * SIDE + lax.rem(y + step_y, SIDE)

    straight = [(0, d) for d in range(1, SIDE)] + [(d, 0) for d in range(1, SIDE)]
    turning = [(a, b) for a in range(1, SIDE) for b in range(1, SIDE)]

    barrier = pltpu.get_barrier_semaphore()
    greetings = jnp.int32(len(straight))
    for step_x, step_y in HALO:
        here = inside(step_x, step_y)
        greetings = greetings + jnp.where(here, 1, 0)

        @pl.when(here)
        def _(step_x=step_x, step_y=step_y):
            pl.semaphore_signal(
                barrier, inc=1, device_id=(i + step_x, j + step_y), device_id_type=MESH
            )

    for steps in straight:
        pl.semaphore_signal(
            barrier, inc=1, device_id=(i, partner(*steps)), device_id_type=MESH
        )

    pick = picked_rows()
    loads[0].wait()
    picked = jnp.dot(pick, feat[...], preferred_element_type=F32)
    for k in range(4):
        face_send[k] = picked[k * FACE : (k + 1) * FACE].astype(BF16)
        first = 4 * FACE + k * BRICKS
        edge = picked[first : first + BRICKS]
        edge_send[k] = jnp.concatenate([edge[:, 0:256], edge[:, 256:512]], 0).astype(BF16)

    pl.semaphore_wait(barrier, greetings)
    copies = []
    for k, (step_x, step_y) in enumerate(HALO):
        if k < 4:
            source, target = face_send.at[k], face_recv.at[k]
        else:
            source, target = edge_send.at[k - 4], edge_recv.at[k - 4]
        copy = pltpu.make_async_remote_copy(
            src_ref=source,
            dst_ref=target,
            send_sem=halo_send.at[k],
            recv_sem=halo_recv.at[k],
            device_id=(i + step_x, j + step_y),
            device_id_type=MESH,
        )
        copies.append((copy, inside(step_x, step_y), inside(-step_x, -step_y)))
        pl.when(copies[-1][1])(copy.start)
    for d in range(1, SIDE):
        pl.semaphore_signal(
            known_sem, inc=1, device_id=(i, partner(0, d)), device_id_type=MESH
        )

    table[0:T_FACE] = feat[...].astype(F32).reshape(T_FACE, EDGE, LANES)
    table[T_ZERO:T_SIZE] = jnp.zeros((EDGE, EDGE, LANES), F32)
    for k in range(2):
        ytab[k, 0:BRICKS] = picked[(2 + k) * FACE : (3 + k) * FACE].reshape(BRICKS, EDGE, LANES)
        ytab[k, Y_ZERO] = jnp.zeros((EDGE, LANES), F32)
    for k in range(4):
        repeat_rows(etab, k, 0, picked, 4 * FACE + k * BRICKS)
        etab[k, E_ZERO] = jnp.zeros((EDGE, LANES), F32)

    loads[2].wait()
    for g in range(BRICKS):
        for tap in range(27):
            sx, sy = tap // 9 - 1, tap // 3 % 3 - 1
            value = ids[g, tap]
            brick = value & 7
            far_x = jnp.where(value >> 3 >> 4 == i, 0, 1)
            far_y = jnp.where((value >> 3) & 15 == j, 0, 1)
            if sx == 0 and sy == 0:
                row, zero = brick * EDGE, T_ZERO
            elif sy == 0:
                edge_x, side = (7, 0) if sx < 0 else (0, 1)
                row = jnp.where(far_x == 0, brick * EDGE + edge_x, T_FACE + side * BRICKS + brick)
                zero = T_ZERO
            elif sx == 0:
                row, zero = far_y * BRICKS + brick, Y_ZERO
            else:
                row, zero = far_x * 16 + far_y * 8 + brick, E_ZERO
            index[g, tap] = jnp.where(value >= 0, row, zero)

    loads[1].wait()
    empty = jnp.zeros((CH, CH), BF16)
    blank = jnp.zeros((CH, 2 * CH), BF16)
    for ty in range(3):
        for tx in range(3):
            w = [conv[tx * 9 + ty * 3 + tz] * jnp.array(0.5, BF16) for tz in range(3)]
            pairs = {
                -1: jnp.concatenate([w[0], empty], 1),
                0: jnp.concatenate([w[1], w[0]], 1),
                1: jnp.concatenate([w[2], w[1]], 1),
                2: jnp.concatenate([empty, w[2]], 1),
            }
            for place_in, depth_in in enumerate((0, 1, 2, 3, 4, -1)):
                for q in range(2):
                    first = tx * BAND + place_in * CH
                    band[ty, first : first + CH, q * 128 : (q + 1) * 128] = pairs.get(
                        depth_in - 2 * q, blank
                    )
    loads[5].wait()
    for a in range(2):
        for b in range(2):
            for k in range(2):
                first = (a * 2 + k) * CH
                down_both[first : first + CH, b * CO : (b + 1) * CO] = down[a * 4 + b * 2 + k]

    loads[3].wait()
    owners = [owner[0, g] for g in range(BRICKS)]
    row, col = iota((8 * CHUNK, FACE * CHUNK), 0), iota((8 * CHUNK, FACE * CHUNK), 1)
    slot_of = jnp.zeros((8 * CHUNK, FACE * CHUNK), jnp.int32)
    for g in range(BRICKS):
        rank = jnp.int32(0)
        for earlier in range(g):
            rank = rank + jnp.where(owners[earlier] == owners[g], 1, 0)
        slot_of = jnp.where((col >> 3) & 7 == g, owners[g] * 2 + rank, slot_of)
    slot_of = jnp.where((col >> 6 == row >> 3) & (col & 7 == (row & 7) * 2), slot_of, -1)
    blocks = [(slot_of == s).astype(F32) for s in range(2 * size_y)]
    place[...] = jnp.concatenate(blocks, 0).astype(BF16)

    loads[4].wait()
    for copy, sent, received in copies:
        pl.when(sent)(copy.wait_send)
        pl.when(received)(copy.wait_recv)
    for k in range(2):
        over_x = face_recv[k].astype(F32)
        over_y = face_recv[2 + k].astype(F32)
        first = T_FACE + k * BRICKS
        table[first : first + BRICKS] = over_x.reshape(BRICKS, EDGE, LANES)
        ytab[k, BRICKS : 2 * BRICKS] = over_y.reshape(BRICKS, EDGE, LANES)
        for side in range(2):
            at = 0 if side else 7
            repeat_rows(etab, side * 2 + k, 8, over_y, at, EDGE)
            repeat_rows(etab, k * 2 + side, 16, over_x, at, EDGE)
            edge = edge_recv[k * 2 + side].astype(F32)
            edge = jnp.concatenate([edge[0:8], edge[8:16]], 1)
            repeat_rows(etab, k * 2 + side, 24, edge)

    low = iota((EDGE, 128), 1) < CH
    last_row = iota((EDGE, BAND), 0) == 7
    first_row = iota((EDGE, BAND), 0) == 0

    def halves(read, centre, minus, plus):
        c = read(centre, 0, LANES)
        m = read(minus, LANES - 128, LANES)
        p = read(plus, 0, 128)
        e0 = jnp.where(low, c[:, 256:384], m)
        e1 = jnp.where(low, p, c[:, 128:256])
        return (
            jnp.concatenate([c[:, 0:256], e0], 1),
            jnp.concatenate([c[:, 256:512], e1], 1),
        )

    def one_slab(g, x):
        sx = -1 if x < 0 else (1 if x > 7 else 0)
        shift = x if sx == 0 else 0
        result = []
        for sy in STEPS:
            tap = (sx + 1) * 9 + (sy + 1) * 3
            if sy == 0:
                def read(row, low_lane, high_lane):
                    return table[row + shift, :, low_lane:high_lane]
            elif sx == 0:
                def read(row, low_lane, high_lane, side=(sy + 1) // 2):
                    lines = ytab[side, row, :, low_lane:high_lane]
                    return pltpu.roll(lines, (7 - x if side == 0 else 0 - x) & 7, 0)
            else:
                def read(row, low_lane, high_lane, corner=(sx + 1) // 2 * 2 + (sy + 1) // 2):
                    return etab[corner, row, :, low_lane:high_lane]
            result.append(halves(read, index[g, tap + 1], index[g, tap], index[g, tap + 2]))
        before, same, after = result
        return [
            [jnp.where(last_row, before[h], same[h]), same[h], jnp.where(first_row, after[h], same[h])]
            for h in range(2)
        ]

    def gather(slabs):
        for x in slabs:
            for pair in range(BRICKS // 2):
                even = one_slab(pair * 2, x)
                odd = one_slab(pair * 2 + 1, x)
                for h in range(2):
                    for ty in range(3):
                        both = jnp.concatenate([even[h][ty], odd[h][ty]], 0)
                        stack[ty, x + 1, h, pair * 16 : pair * 16 + 16] = both.astype(BF16)

    def out_copy(chunk, steps):
        dest = partner(*steps)
        return pltpu.make_async_remote_copy(
            src_ref=stage.at[chunk, pl.ds(dest * 2, 2)],
            dst_ref=out_ref.at[pl.ds(j * 2, 2), pl.ds(chunk * CHUNK, CHUNK)],
            send_sem=out_send.at[chunk, steps[0] * SIDE + steps[1]],
            recv_sem=out_recv.at[chunk, steps[0] * SIDE + steps[1]],
            device_id=(i, dest),
            device_id_type=MESH,
        )

    def own_copy(chunk):
        return pltpu.make_async_copy(
            stage.at[chunk, pl.ds(j * 2, 2)],
            out_ref.at[pl.ds(j * 2, 2), pl.ds(chunk * CHUNK, CHUNK)],
            own_sem.at[chunk],
        )

    bias_row = jnp.concatenate([bias[...] * 0.5] * 4, 1)
    slabs = 2 * CHUNK
    size = slabs * 2 * FACE
    gather([-1, 0])
    for chunk in range(CHUNKS):
        base = chunk * slabs
        gather(range(base + 1, base + slabs + 1))
        total = None
        for ty in range(3):
            window = jnp.concatenate(
                [
                    stack[ty, base + tx : base + tx + slabs].reshape(size, BAND)
                    for tx in range(3)
                ],
                1,
            )
            part = jnp.dot(window, band[ty], preferred_element_type=F32)
            if ty != 1:
                part = pltpu.roll(part.reshape(size // 8, 8, HALF), 1 if ty == 0 else 7, 1)
                part = part.reshape(size, HALF)
            total = part if total is None else total + part
        half_v = total + bias_row
        own = stack[1, base + 1 : base + 1 + slabs, :, :, 0:HALF].reshape(size, HALF)
        hidden = own.astype(F32) + (half_v + half_v * jnp.tanh(half_v))
        hidden = hidden.astype(BF16).reshape(CHUNK, 2, 2 * FACE, HALF)
        lhs = jnp.concatenate(
            [
                jnp.concatenate([hidden[:, a, :, k * 128 : (k + 1) * 128] for a in range(2)], 2)
                for k in range(2)
            ],
            0,
        ).reshape(2 * CHUNK * 2 * FACE, 256)
        coarse = jnp.dot(lhs, down_both[...], preferred_element_type=F32)
        odd = pltpu.roll(coarse[:, CO:].reshape(-1, 8, CO), 7, 1).reshape(-1, CO)
        coarse = (coarse[:, :CO] + odd).astype(BF16).reshape(2, CHUNK, 2, FACE, CO)
        coarse = jnp.concatenate(
            [coarse[k, :, h] for h in range(2) for k in range(2)], 2
        ).reshape(CHUNK * FACE, 4 * CO)
        placed = jnp.dot(place[...], coarse, preferred_element_type=F32)
        placed = placed.reshape(2 * size_y, CHUNK, 8, 4 * CO)[:, :, 0:4]
        stage[chunk] = placed.astype(BF16)
        for steps in straight:
            out_copy(chunk, steps).start()
        if chunk == 0:
            pl.semaphore_wait(known_sem, SIDE - 1)
        for steps in turning:
            out_copy(chunk, steps).start()
        own_copy(chunk).start()
    for chunk in range(CHUNKS):
        for steps in straight + turning:
            out_copy(chunk, steps).wait()
        own_copy(chunk).wait()


def shards(features, neighbour_ids, conv_weight, conv_bias, down_weight, coarse_owner):
    size_x = lax.axis_size("bx")
    size_y = lax.axis_size("by")
    slots = 2 * size_y
    hbm_spec = pl.BlockSpec(memory_space=pltpu.HBM)
    return pl.pallas_call(
        functools.partial(kernel, size_x, size_y),
        out_shape=jax.ShapeDtypeStruct((slots, 4, 4, 4 * CO), BF16),
        in_specs=[hbm_spec] * 6,
        out_specs=pl.BlockSpec(memory_space=pl.ANY),
        scratch_shapes=[
            pltpu.SMEM((BRICKS, 27), jnp.int32),
            pltpu.SMEM((1, BRICKS), jnp.int32),
            pltpu.VMEM((ROWS, LANES), BF16),
            pltpu.VMEM((27, CH, CH), BF16),
            pltpu.VMEM((1, CH), F32),
            pltpu.VMEM((8, CH, CO), BF16),
            pltpu.SMEM((BRICKS, 27), jnp.int32),
            pltpu.VMEM((4, FACE, LANES), BF16),
            pltpu.VMEM((4, 16, 256), BF16),
            pltpu.VMEM((4, FACE, LANES), BF16),
            pltpu.VMEM((4, 16, 256), BF16),
            pltpu.VMEM((T_SIZE, EDGE, LANES), F32),
            pltpu.VMEM((2, Y_SIZE, EDGE, LANES), F32),
            pltpu.VMEM((4, E_SIZE, EDGE, LANES), F32),
            pltpu.VMEM((3, 10, 2, FACE, BAND), BF16),
            pltpu.VMEM((3, 3 * BAND, HALF), BF16),
            pltpu.VMEM((256, 2 * CO), BF16),
            pltpu.VMEM((slots * 8 * CHUNK, FACE * CHUNK), BF16),
            pltpu.VMEM((CHUNKS, slots, CHUNK, 4, 4 * CO), BF16),
            pltpu.SemaphoreType.DMA((6,)),
            pltpu.SemaphoreType.DMA((8,)),
            pltpu.SemaphoreType.DMA((8,)),
            pltpu.SemaphoreType.DMA((CHUNKS, size_y)),
            pltpu.SemaphoreType.DMA((CHUNKS, size_y)),
            pltpu.SemaphoreType.DMA((CHUNKS,)),
            pltpu.SemaphoreType.REGULAR,
        ],
        compiler_params=pltpu.CompilerParams(
            collective_id=0, has_side_effects=True, vmem_limit_bytes=63 * 1024 * 1024
        ),
        name="brick_encoder",
    )(
        neighbour_ids,
        coarse_owner.reshape(1, BRICKS),
        features.reshape(ROWS, LANES),
        conv_weight,
        conv_bias.reshape(1, CH),
        down_weight,
    )


def solution(mesh):
    in_specs = (
        P(("bx", "by"), None, None, None),
        P(("bx", "by"), None),
        P(),
        P(),
        P(),
        P(("bx", "by"), None),
    )
    out_specs = P(("bx", "by"), None, None, None)
    return jax.shard_map(shards, mesh=mesh, in_specs=in_specs, out_specs=out_specs, check_vma=False)
```

```python
import functools

import jax
import jax.numpy as jnp
from jax import lax
from jax.experimental import pallas as pl
from jax.experimental.pallas import tpu as pltpu
from jax.sharding import PartitionSpec as P

MESH = pl.DeviceIdType.MESH
F32 = jnp.float32
BF16 = jnp.bfloat16

EDGE = 8
BRICKS = 8
CH = 64
CO = 128
LANES = EDGE * CH
ROWS = BRICKS * EDGE * EDGE
HALF = 4 * CH
BAND = 6 * CH
FACE = BRICKS * EDGE

T_FACE = BRICKS * EDGE
T_ZERO = T_FACE + 2 * BRICKS
T_SIZE = T_ZERO + EDGE
Y_ZERO = 2 * BRICKS
Y_SIZE = Y_ZERO + 1
E_ZERO = 4 * BRICKS
E_SIZE = E_ZERO + 1

STEPS = (-1, 0, 1)
CHUNK = 2
CHUNKS = EDGE // 2 // CHUNK
SIDE = 4
PARTS = 4
HALO = [(1, 0), (-1, 0), (0, 1), (0, -1), (1, 1), (1, -1), (-1, 1), (-1, -1)]


def iota(shape, dim):
    return lax.broadcasted_iota(jnp.int32, shape, dim)


def picked_rows():
    targets = []
    inner = iota((FACE, 128), 0)
    for first in (56, 0):
        targets.append((inner >> 3) * 64 + first + (inner & 7))
    for first in (7, 0):
        targets.append(inner * 8 + first)
    inner = iota((4 * BRICKS, 128), 0)
    corner = inner >> 3
    targets.append(
        (inner & 7) * 64 + jnp.where(corner < 2, 56, 0) + jnp.where(corner & 1 == 0, 7, 0)
    )
    target = jnp.concatenate(targets, 0)
    target = target - iota(target.shape, 1)
    blocks = [(target == 128 * k).astype(F32) for k in range(ROWS // 128)]
    return jnp.concatenate(blocks, 1).astype(BF16)


def repeat_rows(target, corner, first, rows, start=0, step=1):
    for k in range(BRICKS):
        row = start + step * k
        target[corner, first + k] = jnp.broadcast_to(rows[row : row + 1], (EDGE, LANES))


def kernel(
    size_x, size_y,
    ids_hbm, owner_hbm, feat_hbm, conv_hbm, bias_hbm, down_hbm,
    out_ref,
    ids, owner, feat, conv, bias, down,
    index, face_send, edge_send, face_recv, edge_recv, table, ytab, etab,
    stack, band, down_both, place, stage,
    load_sem, halo_send, halo_recv, out_send, out_recv, own_sem, known_sem,
):
    i = lax.axis_index("bx")
    j = lax.axis_index("by")
    z, y = j // SIDE, lax.rem(j, SIDE)

    loads = [
        pltpu.make_async_copy(source, target, load_sem.at[k])
        for k, (source, target) in enumerate(
            [
                (feat_hbm, feat),
                (conv_hbm, conv),
                (ids_hbm, ids),
                (owner_hbm, owner),
                (bias_hbm, bias),
                (down_hbm, down),
            ]
        )
    ]
    for load in loads:
        load.start()

    def inside(step_x, step_y):
        x_in = (i + step_x >= 0) & (i + step_x < size_x)
        return x_in & (j + step_y >= 0) & (j + step_y < size_y)

    def partner(step_z, step_y):
        return lax.rem(z + step_z, SIDE) * SIDE + lax.rem(y + step_y, SIDE)

    straight = [(0, d) for d in range(1, SIDE)] + [(d, 0) for d in range(1, SIDE)]
    turning = [(a, b) for a in range(1, SIDE) for b in range(1, SIDE)]

    barrier = pltpu.get_barrier_semaphore()
    for steps in straight:
        pl.semaphore_signal(
            barrier, inc=1, device_id=(i, partner(*steps)), device_id_type=MESH
        )
    greetings = jnp.int32(len(straight))
    for step_x, step_y in HALO:
        here = inside(step_x, step_y)
        greetings = greetings + jnp.where(here, 1, 0)

        @pl.when(here)
        def _(step_x=step_x, step_y=step_y):
            pl.semaphore_signal(
                barrier, inc=1, device_id=(i + step_x, j + step_y), device_id_type=MESH
            )

    pick = picked_rows()
    loads[0].wait()
    picked = jnp.dot(pick, feat[...], preferred_element_type=F32)
    for k in range(4):
        face_send[k] = picked[k * FACE : (k + 1) * FACE].astype(BF16)
        first = 4 * FACE + k * BRICKS
        edge = picked[first : first + BRICKS]
        edge_send[k] = jnp.concatenate([edge[:, 0:256], edge[:, 256:512]], 0).astype(BF16)

    pl.semaphore_wait(barrier, greetings)
    copies = []
    for k, (step_x, step_y) in enumerate(HALO):
        if k < 4:
            source, target = face_send.at[k], face_recv.at[k]
        else:
            source, target = edge_send.at[k - 4], edge_recv.at[k - 4]
        copy = pltpu.make_async_remote_copy(
            src_ref=source,
            dst_ref=target,
            send_sem=halo_send.at[k],
            recv_sem=halo_recv.at[k],
            device_id=(i + step_x, j + step_y),
            device_id_type=MESH,
        )
        copies.append((copy, inside(step_x, step_y), inside(-step_x, -step_y)))
    for copy, sent, received in copies[4:] + copies[2:4] + copies[:2]:
        pl.when(sent)(copy.start)
    for d in range(1, SIDE):
        pl.semaphore_signal(
            known_sem, inc=1, device_id=(i, partner(0, d)), device_id_type=MESH
        )

    table[0:T_FACE] = feat[...].astype(F32).reshape(T_FACE, EDGE, LANES)
    table[T_ZERO:T_SIZE] = jnp.zeros((EDGE, EDGE, LANES), F32)
    for k in range(2):
        ytab[k, 0:BRICKS] = picked[(2 + k) * FACE : (3 + k) * FACE].reshape(BRICKS, EDGE, LANES)
        ytab[k, Y_ZERO] = jnp.zeros((EDGE, LANES), F32)
    for k in range(4):
        repeat_rows(etab, k, 0, picked, 4 * FACE + k * BRICKS)
        etab[k, E_ZERO] = jnp.zeros((EDGE, LANES), F32)

    loads[2].wait()
    for g in range(BRICKS):
        for tap in range(27):
            sx, sy = tap // 9 - 1, tap // 3 % 3 - 1
            value = ids[g, tap]
            brick = value & 7
            far_x = jnp.where(value >> 3 >> 4 == i, 0, 1)
            far_y = jnp.where((value >> 3) & 15 == j, 0, 1)
            if sx == 0 and sy == 0:
                row, zero = brick * EDGE, T_ZERO
            elif sy == 0:
                edge_x, side = (7, 0) if sx < 0 else (0, 1)
                row = jnp.where(far_x == 0, brick * EDGE + edge_x, T_FACE + side * BRICKS + brick)
                zero = T_ZERO
            elif sx == 0:
                row, zero = far_y * BRICKS + brick, Y_ZERO
            else:
                row, zero = far_x * 16 + far_y * 8 + brick, E_ZERO
            index[g, tap] = jnp.where(value >= 0, row, zero)

    loads[1].wait()
    empty = jnp.zeros((CH, CH), BF16)
    blank = jnp.zeros((CH, 2 * CH), BF16)
    for ty in range(3):
        for tx in range(3):
            w = [conv[tx * 9 + ty * 3 + tz] * jnp.array(0.5, BF16) for tz in range(3)]
            pairs = {
                -1: jnp.concatenate([w[0], empty], 1),
                0: jnp.concatenate([w[1], w[0]], 1),
                1: jnp.concatenate([w[2], w[1]], 1),
                2: jnp.concatenate([empty, w[2]], 1),
            }
            for place_in, depth_in in enumerate((0, 1, 2, 3, 4, -1)):
                for q in range(2):
                    first = tx * BAND + place_in * CH
                    band[ty, first : first + CH, q * 128 : (q + 1) * 128] = pairs.get(
                        depth_in - 2 * q, blank
                    )
    loads[5].wait()
    for a in range(2):
        for b in range(2):
            for k in range(2):
                first = (a * 2 + k) * CH
                down_both[first : first + CH, b * CO : (b + 1) * CO] = down[a * 4 + b * 2 + k]

    loads[3].wait()
    owners = [owner[0, g] for g in range(BRICKS)]
    row, col = iota((8 * CHUNK, FACE * CHUNK), 0), iota((8 * CHUNK, FACE * CHUNK), 1)
    slot_of = jnp.zeros((8 * CHUNK, FACE * CHUNK), jnp.int32)
    for g in range(BRICKS):
        rank = jnp.int32(0)
        for earlier in range(g):
            rank = rank + jnp.where(owners[earlier] == owners[g], 1, 0)
        slot_of = jnp.where((col >> 3) & 7 == g, owners[g] * 2 + rank, slot_of)
    slot_of = jnp.where((col >> 6 == row >> 3) & (col & 7 == (row & 7) * 2), slot_of, -1)
    blocks = [(slot_of == s).astype(F32) for s in range(2 * size_y)]
    place[...] = jnp.concatenate(blocks, 0).astype(BF16)

    loads[4].wait()
    for copy, sent, received in copies:
        pl.when(sent)(copy.wait_send)
        pl.when(received)(copy.wait_recv)
    for k in range(2):
        over_x = face_recv[k].astype(F32)
        over_y = face_recv[2 + k].astype(F32)
        first = T_FACE + k * BRICKS
        table[first : first + BRICKS] = over_x.reshape(BRICKS, EDGE, LANES)
        ytab[k, BRICKS : 2 * BRICKS] = over_y.reshape(BRICKS, EDGE, LANES)
        for side in range(2):
            at = 0 if side else 7
            repeat_rows(etab, side * 2 + k, 8, over_y, at, EDGE)
            repeat_rows(etab, k * 2 + side, 16, over_x, at, EDGE)
            edge = edge_recv[k * 2 + side].astype(F32)
            edge = jnp.concatenate([edge[0:8], edge[8:16]], 1)
            repeat_rows(etab, k * 2 + side, 24, edge)

    low = iota((EDGE, 128), 1) < CH
    last_row = iota((EDGE, BAND), 0) == 7
    first_row = iota((EDGE, BAND), 0) == 0

    def halves(read, centre, minus, plus):
        c = read(centre, 0, LANES)
        m = read(minus, LANES - 128, LANES)
        p = read(plus, 0, 128)
        e0 = jnp.where(low, c[:, 256:384], m)
        e1 = jnp.where(low, p, c[:, 128:256])
        return (
            jnp.concatenate([c[:, 0:256], e0], 1),
            jnp.concatenate([c[:, 256:512], e1], 1),
        )

    def one_slab(g, x):
        sx = -1 if x < 0 else (1 if x > 7 else 0)
        shift = x if sx == 0 else 0
        result = []
        for sy in STEPS:
            tap = (sx + 1) * 9 + (sy + 1) * 3
            if sy == 0:
                def read(row, low_lane, high_lane):
                    return table[row + shift, :, low_lane:high_lane]
            elif sx == 0:
                def read(row, low_lane, high_lane, side=(sy + 1) // 2):
                    lines = ytab[side, row, :, low_lane:high_lane]
                    return pltpu.roll(lines, (7 - x if side == 0 else 0 - x) & 7, 0)
            else:
                def read(row, low_lane, high_lane, corner=(sx + 1) // 2 * 2 + (sy + 1) // 2):
                    return etab[corner, row, :, low_lane:high_lane]
            result.append(halves(read, index[g, tap + 1], index[g, tap], index[g, tap + 2]))
        before, same, after = result
        return [
            [jnp.where(last_row, before[h], same[h]), same[h], jnp.where(first_row, after[h], same[h])]
            for h in range(2)
        ]

    def gather(slabs):
        for x in slabs:
            for pair in range(BRICKS // 2):
                even = one_slab(pair * 2, x)
                odd = one_slab(pair * 2 + 1, x)
                for h in range(2):
                    for ty in range(3):
                        both = jnp.concatenate([even[h][ty], odd[h][ty]], 0)
                        stack[ty, x + 1, h, pair * 16 : pair * 16 + 16] = both.astype(BF16)

    def out_copy(chunk, steps):
        dest = partner(*steps)
        return pltpu.make_async_remote_copy(
            src_ref=stage.at[chunk, pl.ds(dest * 2, 2)],
            dst_ref=out_ref.at[pl.ds(j * 2, 2), pl.ds(chunk * CHUNK, CHUNK)],
            send_sem=out_send.at[chunk, steps[0] * SIDE + steps[1]],
            recv_sem=out_recv.at[chunk, steps[0] * SIDE + steps[1]],
            device_id=(i, dest),
            device_id_type=MESH,
        )

    def own_copy(chunk):
        return pltpu.make_async_copy(
            stage.at[chunk, pl.ds(j * 2, 2)],
            out_ref.at[pl.ds(j * 2, 2), pl.ds(chunk * CHUNK, CHUNK)],
            own_sem.at[chunk],
        )

    bias_row = jnp.concatenate([bias[...] * 0.5] * 4, 1)
    slabs = 2 * CHUNK
    size = slabs * 2 * FACE

    def convolved(chunk, ty):
        base = chunk * slabs
        window = jnp.concatenate(
            [stack[ty, base + tx : base + tx + slabs].reshape(size, BAND) for tx in range(3)], 1
        )
        part = jnp.dot(window, band[ty], preferred_element_type=F32)
        if ty != 1:
            part = pltpu.roll(part.reshape(size // 8, 8, HALF), 1 if ty == 0 else 7, 1)
            part = part.reshape(size, HALF)
        return part

    def reduced(chunk, total):
        base = chunk * slabs
        half_v = total + bias_row
        own = stack[1, base + 1 : base + 1 + slabs, :, :, 0:HALF].reshape(size, HALF)
        hidden = own.astype(F32) + (half_v + half_v * jnp.tanh(half_v))
        hidden = hidden.astype(BF16).reshape(CHUNK, 2, 2 * FACE, HALF)
        lhs = jnp.concatenate(
            [
                jnp.concatenate([hidden[:, a, :, k * 128 : (k + 1) * 128] for a in range(2)], 2)
                for k in range(2)
            ],
            0,
        ).reshape(2 * CHUNK * 2 * FACE, 256)
        coarse = jnp.dot(lhs, down_both[...], preferred_element_type=F32)
        odd = pltpu.roll(coarse[:, CO:].reshape(-1, 8, CO), 7, 1).reshape(-1, CO)
        coarse = (coarse[:, :CO] + odd).astype(BF16).reshape(2, CHUNK, 2, FACE, CO)
        return jnp.concatenate(
            [coarse[k, :, h] for h in range(2) for k in range(2)], 2
        ).reshape(CHUNK * FACE, 4 * CO)

    def staged(chunk, coarse):
        placed = jnp.dot(place[...], coarse, preferred_element_type=F32)
        placed = placed.reshape(2 * size_y, CHUNK, 8, 4 * CO)[:, :, 0:4]
        stage[chunk] = placed.astype(BF16)

    def send(chunk):
        if chunk == 0:
            pl.semaphore_wait(known_sem, SIDE - 1)
        for steps in turning + straight:
            out_copy(chunk, steps).start()
        own_copy(chunk).start()

    gather([-1, 0])
    for chunk in range(CHUNKS):
        gather(range(chunk * slabs + 1, chunk * slabs + slabs + 1))
        total = convolved(chunk, 0) + convolved(chunk, 1) + convolved(chunk, 2)
        staged(chunk, reduced(chunk, total))
        send(chunk)
    for chunk in range(CHUNKS):
        for steps in straight + turning:
            out_copy(chunk, steps).wait()
        own_copy(chunk).wait()


def hand_over(source, target, held, in_sem, out_sem):
    size = source.shape[0] // PARTS
    ins, outs = [], []
    for k in range(PARTS):
        part = pl.ds(k * size, size)
        ins.append(pltpu.make_async_copy(source.at[part], held.at[part], in_sem.at[k]))
        outs.append(pltpu.make_async_copy(held.at[part], target.at[part], out_sem.at[k]))
    for copy in ins:
        copy.start()
    for arrived, leaving in zip(ins, outs):
        arrived.wait()
        leaving.start()
    for copy in outs:
        copy.wait()


def shards(features, neighbour_ids, conv_weight, conv_bias, down_weight, coarse_owner):
    size_x = lax.axis_size("bx")
    size_y = lax.axis_size("by")
    slots = 2 * size_y
    hbm_spec = pl.BlockSpec(memory_space=pltpu.HBM)
    out = pl.pallas_call(
        functools.partial(kernel, size_x, size_y),
        out_shape=jax.ShapeDtypeStruct((slots, 4, 4, 4 * CO), BF16),
        in_specs=[hbm_spec] * 6,
        out_specs=pl.BlockSpec(memory_space=pl.ANY),
        scratch_shapes=[
            pltpu.SMEM((BRICKS, 27), jnp.int32),
            pltpu.SMEM((1, BRICKS), jnp.int32),
            pltpu.VMEM((ROWS, LANES), BF16),
            pltpu.VMEM((27, CH, CH), BF16),
            pltpu.VMEM((1, CH), F32),
            pltpu.VMEM((8, CH, CO), BF16),
            pltpu.SMEM((BRICKS, 27), jnp.int32),
            pltpu.VMEM((4, FACE, LANES), BF16),
            pltpu.VMEM((4, 16, 256), BF16),
            pltpu.VMEM((4, FACE, LANES), BF16),
            pltpu.VMEM((4, 16, 256), BF16),
            pltpu.VMEM((T_SIZE, EDGE, LANES), F32),
            pltpu.VMEM((2, Y_SIZE, EDGE, LANES), F32),
            pltpu.VMEM((4, E_SIZE, EDGE, LANES), F32),
            pltpu.VMEM((3, 10, 2, FACE, BAND), BF16),
            pltpu.VMEM((3, 3 * BAND, HALF), BF16),
            pltpu.VMEM((256, 2 * CO), BF16),
            pltpu.VMEM((slots * 8 * CHUNK, FACE * CHUNK), BF16),
            pltpu.VMEM((CHUNKS, slots, CHUNK, 4, 4 * CO), BF16),
            pltpu.SemaphoreType.DMA((6,)),
            pltpu.SemaphoreType.DMA((8,)),
            pltpu.SemaphoreType.DMA((8,)),
            pltpu.SemaphoreType.DMA((CHUNKS, size_y)),
            pltpu.SemaphoreType.DMA((CHUNKS, size_y)),
            pltpu.SemaphoreType.DMA((CHUNKS,)),
            pltpu.SemaphoreType.REGULAR,
        ],
        compiler_params=pltpu.CompilerParams(
            collective_id=0, has_side_effects=True, vmem_limit_bytes=63 * 1024 * 1024
        ),
        name="brick_encoder",
    )(
        neighbour_ids,
        coarse_owner.reshape(1, BRICKS),
        features.reshape(ROWS, LANES),
        conv_weight,
        conv_bias.reshape(1, CH),
        down_weight,
    )
    return pl.pallas_call(
        hand_over,
        out_shape=jax.ShapeDtypeStruct(out.shape, out.dtype),
        in_specs=[pl.BlockSpec(memory_space=pl.ANY)],
        out_specs=pl.BlockSpec(memory_space=pl.ANY),
        scratch_shapes=[
            pltpu.VMEM(out.shape, out.dtype),
            pltpu.SemaphoreType.DMA((PARTS,)),
            pltpu.SemaphoreType.DMA((PARTS,)),
        ],
        compiler_params=pltpu.CompilerParams(vmem_limit_bytes=63 * 1024 * 1024),
        name="hand_over",
    )(out)


def solution(mesh):
    in_specs = (
        P(("bx", "by"), None, None, None),
        P(("bx", "by"), None),
        P(),
        P(),
        P(),
        P(("bx", "by"), None),
    )
    out_specs = P(("bx", "by"), None, None, None)
    return jax.shard_map(shards, mesh=mesh, in_specs=in_specs, out_specs=out_specs, check_vma=False)
```

```python
import functools

import jax
import jax.numpy as jnp
from jax import lax
from jax.experimental import pallas as pl
from jax.experimental.pallas import tpu as pltpu
from jax.sharding import PartitionSpec as P

MESH = pl.DeviceIdType.MESH
F32 = jnp.float32
BF16 = jnp.bfloat16

EDGE = 8
BRICKS = 8
CH = 64
CO = 128
LANES = EDGE * CH
ROWS = BRICKS * EDGE * EDGE
HALF = 4 * CH
BAND = 6 * CH
FACE = BRICKS * EDGE

T_FACE = BRICKS * EDGE
T_ZERO = T_FACE + 2 * BRICKS
T_SIZE = T_ZERO + EDGE
Y_ZERO = 2 * BRICKS
Y_SIZE = Y_ZERO + 1
E_ZERO = 4 * BRICKS
E_SIZE = E_ZERO + 1

STEPS = (-1, 0, 1)
CHUNK = 2
CHUNKS = EDGE // 2 // CHUNK
SIDE = 4
PARTS = 4
HALO = [(1, 0), (-1, 0), (0, 1), (0, -1), (1, 1), (1, -1), (-1, 1), (-1, -1)]


def iota(shape, dim):
    return lax.broadcasted_iota(jnp.int32, shape, dim)


def picked_rows():
    targets = []
    inner = iota((FACE, 128), 0)
    for first in (56, 0):
        targets.append((inner >> 3) * 64 + first + (inner & 7))
    for first in (7, 0):
        targets.append(inner * 8 + first)
    inner = iota((4 * BRICKS, 128), 0)
    corner = inner >> 3
    targets.append(
        (inner & 7) * 64 + jnp.where(corner < 2, 56, 0) + jnp.where(corner & 1 == 0, 7, 0)
    )
    target = jnp.concatenate(targets, 0)
    target = target - iota(target.shape, 1)
    blocks = [(target == 128 * k).astype(F32) for k in range(ROWS // 128)]
    return jnp.concatenate(blocks, 1).astype(BF16)


def repeat_rows(target, corner, first, rows, start=0, step=1):
    for k in range(BRICKS):
        row = start + step * k
        target[corner, first + k] = jnp.broadcast_to(rows[row : row + 1], (EDGE, LANES))


def kernel(
    size_x, size_y,
    ids_hbm, owner_hbm, feat_hbm, conv_hbm, bias_hbm, down_hbm,
    out_ref,
    ids, owner, feat, conv, bias, down,
    index, face_send, edge_send, face_recv, edge_recv, table, ytab, etab,
    stack, outer, lines, columns, acc, band, down_both, place, spread, stage,
    load_sem, halo_send, halo_recv, out_send, out_recv, own_sem, known_sem,
):
    i = lax.axis_index("bx")
    j = lax.axis_index("by")
    z, y = j // SIDE, lax.rem(j, SIDE)

    loads = [
        pltpu.make_async_copy(source, target, load_sem.at[k])
        for k, (source, target) in enumerate(
            [
                (feat_hbm, feat),
                (conv_hbm, conv),
                (ids_hbm, ids),
                (owner_hbm, owner),
                (bias_hbm, bias),
                (down_hbm, down),
            ]
        )
    ]
    for load in loads:
        load.start()

    def inside(step_x, step_y):
        x_in = (i + step_x >= 0) & (i + step_x < size_x)
        return x_in & (j + step_y >= 0) & (j + step_y < size_y)

    def partner(step_z, step_y):
        return lax.rem(z + step_z, SIDE) * SIDE + lax.rem(y + step_y, SIDE)

    straight = [(0, d) for d in range(1, SIDE)] + [(d, 0) for d in range(1, SIDE)]
    turning = [(a, b) for a in range(1, SIDE) for b in range(1, SIDE)]

    barrier = pltpu.get_barrier_semaphore()
    for steps in straight:
        pl.semaphore_signal(
            barrier, inc=1, device_id=(i, partner(*steps)), device_id_type=MESH
        )
    greetings = jnp.int32(len(straight))
    for step_x, step_y in HALO:
        here = inside(step_x, step_y)
        greetings = greetings + jnp.where(here, 1, 0)

        @pl.when(here)
        def _(step_x=step_x, step_y=step_y):
            pl.semaphore_signal(
                barrier, inc=1, device_id=(i + step_x, j + step_y), device_id_type=MESH
            )

    pick = picked_rows()
    loads[0].wait()
    picked = jnp.dot(pick, feat[...], preferred_element_type=F32)
    for k in range(4):
        face_send[k] = picked[k * FACE : (k + 1) * FACE].astype(BF16)
        first = 4 * FACE + k * BRICKS
        edge = picked[first : first + BRICKS]
        edge_send[k] = jnp.concatenate([edge[:, 0:256], edge[:, 256:512]], 0).astype(BF16)

    pl.semaphore_wait(barrier, greetings)
    copies = []
    for k, (step_x, step_y) in enumerate(HALO):
        if k < 4:
            source, target = face_send.at[k], face_recv.at[k]
        else:
            source, target = edge_send.at[k - 4], edge_recv.at[k - 4]
        copy = pltpu.make_async_remote_copy(
            src_ref=source,
            dst_ref=target,
            send_sem=halo_send.at[k],
            recv_sem=halo_recv.at[k],
            device_id=(i + step_x, j + step_y),
            device_id_type=MESH,
        )
        copies.append((copy, inside(step_x, step_y), inside(-step_x, -step_y)))
    for copy, sent, received in copies[4:] + copies[2:4] + copies[:2]:
        pl.when(sent)(copy.start)
    for d in range(1, SIDE):
        pl.semaphore_signal(
            known_sem, inc=1, device_id=(i, partner(0, d)), device_id_type=MESH
        )

    table[0:T_FACE] = feat[...].astype(F32).reshape(T_FACE, EDGE, LANES)
    table[T_ZERO:T_SIZE] = jnp.zeros((EDGE, EDGE, LANES), F32)
    loads[2].wait()

    def locate(bricks, taps):
        for g in bricks:
            for tap in taps:
                sx, sy = tap // 9 - 1, tap // 3 % 3 - 1
                value = ids[g, tap]
                brick = value & 7
                far_x = jnp.where(value >> 3 >> 4 == i, 0, 1)
                far_y = jnp.where((value >> 3) & 15 == j, 0, 1)
                if sx == 0 and sy == 0:
                    row, zero = brick * EDGE, T_ZERO
                elif sy == 0:
                    edge_x, side = (7, 0) if sx < 0 else (0, 1)
                    row = jnp.where(
                        far_x == 0, brick * EDGE + edge_x, T_FACE + side * BRICKS + brick
                    )
                    zero = T_ZERO
                elif sx == 0:
                    row, zero = far_y * BRICKS + brick, Y_ZERO
                else:
                    row, zero = far_x * 16 + far_y * 8 + brick, E_ZERO
                index[g, tap] = jnp.where(value >= 0, row, zero)

    locate(range(BRICKS), (12, 14))

    loads[1].wait()
    empty = jnp.zeros((CH, CH), BF16)
    blank = jnp.zeros((CH, 2 * CH), BF16)
    for ty in range(3):
        for tx in range(3):
            w = [conv[tx * 9 + ty * 3 + tz] * jnp.array(0.5, BF16) for tz in range(3)]
            pairs = {
                -1: jnp.concatenate([w[0], empty], 1),
                0: jnp.concatenate([w[1], w[0]], 1),
                1: jnp.concatenate([w[2], w[1]], 1),
                2: jnp.concatenate([empty, w[2]], 1),
            }
            for place_in, depth_in in enumerate((0, 1, 2, 3, 4, -1)):
                for q in range(2):
                    first = tx * BAND + place_in * CH
                    band[ty, first : first + CH, q * 128 : (q + 1) * 128] = pairs.get(
                        depth_in - 2 * q, blank
                    )
    loads[5].wait()
    for a in range(2):
        for b in range(2):
            for k in range(2):
                first = (a * 2 + k) * CH
                down_both[first : first + CH, b * CO : (b + 1) * CO] = down[a * 4 + b * 2 + k]

    low = iota((EDGE, 128), 1) < CH

    def halves(c, m, p):
        e0 = jnp.where(low, c[:, 256:384], m)
        e1 = jnp.where(low, p, c[:, 128:256])
        return (
            jnp.concatenate([c[:, 0:256], e0], 1),
            jnp.concatenate([c[:, 256:512], e1], 1),
        )

    def local_slab(g, x):
        return halves(
            table[g * EDGE + x],
            table[index[g, 12] + x, :, LANES - 128 : LANES],
            table[index[g, 14] + x, :, 0:128],
        )

    stack[0] = jnp.zeros((2, FACE, BAND), BF16)
    stack[9] = jnp.zeros((2, FACE, BAND), BF16)
    for k in range(2):
        columns[k, 0] = jnp.zeros((16, BAND), BF16)
        columns[k, 9] = jnp.zeros((16, BAND), BF16)

    def gather_local(slabs):
        for x in slabs:
            for pair in range(BRICKS // 2):
                even, odd = local_slab(pair * 2, x), local_slab(pair * 2 + 1, x)
                for h in range(2):
                    both = jnp.concatenate([even[h], odd[h]], 0)
                    stack[x + 1, h, pair * 16 : pair * 16 + 16] = both.astype(BF16)

    def windows(source, first, count, rows):
        return jnp.concatenate(
            [source[first + tx : first + tx + count].reshape(rows, BAND) for tx in range(3)], 1
        )

    def shifted(part, ty):
        if ty == 1:
            return part
        moved = pltpu.roll(part.reshape(-1, 8, HALF), 1 if ty == 0 else 7, 1)
        return moved.reshape(part.shape)

    def convolve_local(first, count):
        rows = count * 2 * FACE
        window = windows(stack, first, count, rows)
        y_of = iota((rows, HALF), 0) & 7
        total = jnp.dot(window, band[1], preferred_element_type=F32)
        for ty, empty in ((0, 0), (2, 7)):
            part = jnp.dot(window, band[ty], preferred_element_type=F32)
            total = total + jnp.where(y_of == empty, 0.0, shifted(part, ty))
        acc[first : first + count] = total.reshape(count, 2, FACE, HALF)

    rest = [tap for tap in range(27) if tap not in (12, 13, 14)]
    gather_local(range(0, 5))
    convolve_local(0, 4)
    locate(range(0, 4), rest)
    gather_local(range(5, 8))
    convolve_local(4, 4)
    locate(range(4, 8), rest)

    for k in range(2):
        ytab[k, 0:BRICKS] = picked[(2 + k) * FACE : (3 + k) * FACE].reshape(BRICKS, EDGE, LANES)
        ytab[k, Y_ZERO] = jnp.zeros((EDGE, LANES), F32)
    for k in range(4):
        repeat_rows(etab, k, 0, picked, 4 * FACE + k * BRICKS)
        etab[k, E_ZERO] = jnp.zeros((EDGE, LANES), F32)

    loads[3].wait()
    owners = [owner[0, g] for g in range(BRICKS)]
    row, col = iota((8 * CHUNK, FACE * CHUNK), 0), iota((8 * CHUNK, FACE * CHUNK), 1)
    slot_of = jnp.zeros((8 * CHUNK, FACE * CHUNK), jnp.int32)
    for g in range(BRICKS):
        rank = jnp.int32(0)
        for earlier in range(g):
            rank = rank + jnp.where(owners[earlier] == owners[g], 1, 0)
        slot_of = jnp.where((col >> 3) & 7 == g, owners[g] * 2 + rank, slot_of)
    slot_of = jnp.where((col >> 6 == row >> 3) & (col & 7 == (row & 7) * 2), slot_of, -1)
    blocks = [(slot_of == s).astype(F32) for s in range(2 * size_y)]
    place[...] = jnp.concatenate(blocks, 0).astype(BF16)

    row, col = iota((128, 128), 0), iota((128, 128), 1)
    turned = ((row >> 3) & 1) * 64 + (row & 7) * 8 + (row >> 4) == col
    turned = turned.astype(F32).astype(BF16)
    count = 2 * CHUNK * 16
    row, col = iota((count * 8, count * 4), 0), iota((count * 8, count * 4), 1)
    wanted = (col // (2 * count)) * 7
    spread[...] = (
        ((row >> 3 == lax.rem(col, count)) & (row & 7 == wanted)).astype(F32).astype(BF16)
    )

    loads[4].wait()
    for copy, sent, received in copies:
        pl.when(sent)(copy.wait_send)
        pl.when(received)(copy.wait_recv)
    for k in range(2):
        over_x = face_recv[k].astype(F32)
        over_y = face_recv[2 + k].astype(F32)
        first = T_FACE + k * BRICKS
        table[first : first + BRICKS] = over_x.reshape(BRICKS, EDGE, LANES)
        ytab[k, BRICKS : 2 * BRICKS] = over_y.reshape(BRICKS, EDGE, LANES)
        for side in range(2):
            at = 0 if side else 7
            repeat_rows(etab, side * 2 + k, 8, over_y, at, EDGE)
            repeat_rows(etab, k * 2 + side, 16, over_x, at, EDGE)
            edge = edge_recv[k * 2 + side].astype(F32)
            edge = jnp.concatenate([edge[0:8], edge[8:16]], 1)
            repeat_rows(etab, k * 2 + side, 24, edge)

    last_row = iota((EDGE, BAND), 0) == 7
    first_row = iota((EDGE, BAND), 0) == 0

    def outer_slab(g, side):
        sx = side * 2 - 1
        result = []
        for sy in STEPS:
            tap = (sx + 1) * 9 + (sy + 1) * 3
            source = table if sy == 0 else etab.at[side * 2 + (sy + 1) // 2]
            result.append(
                halves(
                    source[index[g, tap + 1]],
                    source[index[g, tap], :, LANES - 128 : LANES],
                    source[index[g, tap + 2], :, 0:128],
                )
            )
        before, same, after = result
        return [
            [
                jnp.where(last_row, before[h], same[h]),
                same[h],
                jnp.where(first_row, after[h], same[h]),
            ]
            for h in range(2)
        ]

    def line(g, side):
        tap = 9 + side * 6
        return halves(
            ytab[side, index[g, tap + 1]],
            ytab[side, index[g, tap], :, LANES - 128 : LANES],
            ytab[side, index[g, tap + 2], :, 0:128],
        )

    for side in range(2):
        for pair in range(BRICKS // 2):
            even, odd = line(pair * 2, side), line(pair * 2 + 1, side)
            for h in range(2):
                first = h * FACE + pair * 16
                both = jnp.concatenate([even[h], odd[h]], 0)
                lines[side, first : first + 16] = both.astype(BF16)
    for side in range(2):
        moved = jnp.dot(turned, lines[side], preferred_element_type=F32)
        columns[side, 1:9] = moved.astype(BF16).reshape(8, 16, BAND)
    for side in range(2):
        for pair in range(BRICKS // 2):
            even, odd = outer_slab(pair * 2, side), outer_slab(pair * 2 + 1, side)
            for h in range(2):
                for ty in range(3):
                    both = jnp.concatenate([even[h][ty], odd[h][ty]], 0)
                    outer[side, ty, h, pair * 16 : pair * 16 + 16] = both.astype(BF16)
    terms = []
    for side in range(2):
        window = windows(columns.at[side], 0, 8, 128)
        value = jnp.dot(window, band[side * 2], preferred_element_type=F32)
        high = value.astype(BF16)
        terms.append((high, (value - high.astype(F32)).astype(BF16)))
    for side in range(2):
        extra = None
        for ty in range(3):
            first = side * 2 * BAND
            part = jnp.dot(
                outer[side, ty].reshape(2 * FACE, BAND),
                band[ty, first : first + BAND],
                preferred_element_type=F32,
            )
            part = shifted(part, ty)
            extra = part if extra is None else extra + part
        acc[side * 7] = acc[side * 7] + extra.reshape(2, FACE, HALF)

    def convolved(chunk):
        first = chunk * count
        part = jnp.concatenate(
            [term[first : first + count] for pair in terms for term in pair], 0
        )
        total = acc[chunk * slabs : chunk * slabs + slabs].reshape(size, HALF)
        return total + jnp.dot(spread[...], part, preferred_element_type=F32)

    slabs = 2 * CHUNK
    size = slabs * 2 * FACE

    def out_copy(chunk, steps):
        dest = partner(*steps)
        return pltpu.make_async_remote_copy(
            src_ref=stage.at[chunk, pl.ds(dest * 2, 2)],
            dst_ref=out_ref.at[pl.ds(j * 2, 2), pl.ds(chunk * CHUNK, CHUNK)],
            send_sem=out_send.at[chunk, steps[0] * SIDE + steps[1]],
            recv_sem=out_recv.at[chunk, steps[0] * SIDE + steps[1]],
            device_id=(i, dest),
            device_id_type=MESH,
        )

    def own_copy(chunk):
        return pltpu.make_async_copy(
            stage.at[chunk, pl.ds(j * 2, 2)],
            out_ref.at[pl.ds(j * 2, 2), pl.ds(chunk * CHUNK, CHUNK)],
            own_sem.at[chunk],
        )

    bias_row = jnp.concatenate([bias[...] * 0.5] * 4, 1)
    def reduced(chunk, total):
        base = chunk * slabs
        half_v = total + bias_row
        own = stack[base + 1 : base + 1 + slabs, :, :, 0:HALF].reshape(size, HALF)
        hidden = own.astype(F32) + (half_v + half_v * jnp.tanh(half_v))
        hidden = hidden.astype(BF16).reshape(CHUNK, 2, 2 * FACE, HALF)
        lhs = jnp.concatenate(
            [
                jnp.concatenate([hidden[:, a, :, k * 128 : (k + 1) * 128] for a in range(2)], 2)
                for k in range(2)
            ],
            0,
        ).reshape(2 * CHUNK * 2 * FACE, 256)
        coarse = jnp.dot(lhs, down_both[...], preferred_element_type=F32)
        odd = pltpu.roll(coarse[:, CO:].reshape(-1, 8, CO), 7, 1).reshape(-1, CO)
        coarse = (coarse[:, :CO] + odd).astype(BF16).reshape(2, CHUNK, 2, FACE, CO)
        return jnp.concatenate(
            [coarse[k, :, h] for h in range(2) for k in range(2)], 2
        ).reshape(CHUNK * FACE, 4 * CO)

    def staged(chunk, coarse):
        placed = jnp.dot(place[...], coarse, preferred_element_type=F32)
        placed = placed.reshape(2 * size_y, CHUNK, 8, 4 * CO)[:, :, 0:4]
        stage[chunk] = placed.astype(BF16)

    def send(chunk):
        if chunk == 0:
            pl.semaphore_wait(known_sem, SIDE - 1)
        for steps in turning + straight:
            out_copy(chunk, steps).start()
        own_copy(chunk).start()

    for chunk in range(CHUNKS):
        staged(chunk, reduced(chunk, convolved(chunk)))
        send(chunk)
    for chunk in range(CHUNKS):
        for steps in straight + turning:
            out_copy(chunk, steps).wait()
        own_copy(chunk).wait()


def hand_over(source, target, held, in_sem, out_sem):
    size = source.shape[0] // PARTS
    ins, outs = [], []
    for k in range(PARTS):
        part = pl.ds(k * size, size)
        ins.append(pltpu.make_async_copy(source.at[part], held.at[part], in_sem.at[k]))
        outs.append(pltpu.make_async_copy(held.at[part], target.at[part], out_sem.at[k]))
    for copy in ins:
        copy.start()
    for arrived, leaving in zip(ins, outs):
        arrived.wait()
        leaving.start()
    for copy in outs:
        copy.wait()


def shards(features, neighbour_ids, conv_weight, conv_bias, down_weight, coarse_owner):
    size_x = lax.axis_size("bx")
    size_y = lax.axis_size("by")
    slots = 2 * size_y
    hbm_spec = pl.BlockSpec(memory_space=pltpu.HBM)
    out = pl.pallas_call(
        functools.partial(kernel, size_x, size_y),
        out_shape=jax.ShapeDtypeStruct((slots, 4, 4, 4 * CO), BF16),
        in_specs=[hbm_spec] * 6,
        out_specs=pl.BlockSpec(memory_space=pl.ANY),
        scratch_shapes=[
            pltpu.SMEM((BRICKS, 27), jnp.int32),
            pltpu.SMEM((1, BRICKS), jnp.int32),
            pltpu.VMEM((ROWS, LANES), BF16),
            pltpu.VMEM((27, CH, CH), BF16),
            pltpu.VMEM((1, CH), F32),
            pltpu.VMEM((8, CH, CO), BF16),
            pltpu.SMEM((BRICKS, 27), jnp.int32),
            pltpu.VMEM((4, FACE, LANES), BF16),
            pltpu.VMEM((4, 16, 256), BF16),
            pltpu.VMEM((4, FACE, LANES), BF16),
            pltpu.VMEM((4, 16, 256), BF16),
            pltpu.VMEM((T_SIZE, EDGE, LANES), F32),
            pltpu.VMEM((2, Y_SIZE, EDGE, LANES), F32),
            pltpu.VMEM((4, E_SIZE, EDGE, LANES), F32),
            pltpu.VMEM((10, 2, FACE, BAND), BF16),
            pltpu.VMEM((2, 3, 2, FACE, BAND), BF16),
            pltpu.VMEM((2, 2 * FACE, BAND), BF16),
            pltpu.VMEM((2, 10, 16, BAND), BF16),
            pltpu.VMEM((EDGE, 2, FACE, HALF), F32),
            pltpu.VMEM((3, 3 * BAND, HALF), BF16),
            pltpu.VMEM((256, 2 * CO), BF16),
            pltpu.VMEM((slots * 8 * CHUNK, FACE * CHUNK), BF16),
            pltpu.VMEM((256 * CHUNK, 128 * CHUNK), BF16),
            pltpu.VMEM((CHUNKS, slots, CHUNK, 4, 4 * CO), BF16),
            pltpu.SemaphoreType.DMA((6,)),
            pltpu.SemaphoreType.DMA((8,)),
            pltpu.SemaphoreType.DMA((8,)),
            pltpu.SemaphoreType.DMA((CHUNKS, size_y)),
            pltpu.SemaphoreType.DMA((CHUNKS, size_y)),
            pltpu.SemaphoreType.DMA((CHUNKS,)),
            pltpu.SemaphoreType.REGULAR,
        ],
        compiler_params=pltpu.CompilerParams(
            collective_id=0, has_side_effects=True, vmem_limit_bytes=63 * 1024 * 1024
        ),
        name="brick_encoder",
    )(
        neighbour_ids,
        coarse_owner.reshape(1, BRICKS),
        features.reshape(ROWS, LANES),
        conv_weight,
        conv_bias.reshape(1, CH),
        down_weight,
    )
    return pl.pallas_call(
        hand_over,
        out_shape=jax.ShapeDtypeStruct(out.shape, out.dtype),
        in_specs=[pl.BlockSpec(memory_space=pl.ANY)],
        out_specs=pl.BlockSpec(memory_space=pl.ANY),
        scratch_shapes=[
            pltpu.VMEM(out.shape, out.dtype),
            pltpu.SemaphoreType.DMA((PARTS,)),
            pltpu.SemaphoreType.DMA((PARTS,)),
        ],
        compiler_params=pltpu.CompilerParams(vmem_limit_bytes=63 * 1024 * 1024),
        name="hand_over",
    )(out)


def solution(mesh):
    in_specs = (
        P(("bx", "by"), None, None, None),
        P(("bx", "by"), None),
        P(),
        P(),
        P(),
        P(("bx", "by"), None),
    )
    out_specs = P(("bx", "by"), None, None, None)
    return jax.shard_map(shards, mesh=mesh, in_specs=in_specs, out_specs=out_specs, check_vma=False)
```

```python
import functools

import jax
import jax.numpy as jnp
from jax import lax
from jax.experimental import pallas as pl
from jax.experimental.pallas import tpu as pltpu
from jax.sharding import PartitionSpec as P

MESH = pl.DeviceIdType.MESH
F32 = jnp.float32
BF16 = jnp.bfloat16

EDGE = 8
BRICKS = 8
CH = 64
CO = 128
LANES = EDGE * CH
ROWS = BRICKS * EDGE * EDGE
HALF = 4 * CH
BAND = 6 * CH
FACE = BRICKS * EDGE

T_FACE = BRICKS * EDGE
T_ZERO = T_FACE + 2 * BRICKS
T_SIZE = T_ZERO + EDGE
Y_ZERO = 2 * BRICKS
Y_SIZE = Y_ZERO + 1
E_ZERO = 4 * BRICKS
E_SIZE = E_ZERO + 1

STEPS = (-1, 0, 1)
CHUNK = 2
CHUNKS = EDGE // 2 // CHUNK
ORDER = (1, 2, 0, 3)
SIDE = 4
HALO = [(1, 0), (-1, 0), (0, 1), (0, -1), (1, 1), (1, -1), (-1, 1), (-1, -1)]


def iota(shape, dim):
    return lax.broadcasted_iota(jnp.int32, shape, dim)


def picked_rows():
    targets = []
    inner = iota((FACE, 128), 0)
    for first in (56, 0):
        targets.append((inner >> 3) * 64 + first + (inner & 7))
    for first in (7, 0):
        targets.append(inner * 8 + first)
    inner = iota((4 * BRICKS, 128), 0)
    corner = inner >> 3
    targets.append(
        (inner & 7) * 64 + jnp.where(corner < 2, 56, 0) + jnp.where(corner & 1 == 0, 7, 0)
    )
    target = jnp.concatenate(targets, 0)
    target = target - iota(target.shape, 1)
    blocks = [(target == 128 * k).astype(F32) for k in range(ROWS // 128)]
    return jnp.concatenate(blocks, 1).astype(BF16)


def repeat_rows(target, corner, first, rows, start=0, step=1):
    for k in range(BRICKS):
        row = start + step * k
        target[corner, first + k] = jnp.broadcast_to(rows[row : row + 1], (EDGE, LANES))


def kernel(
    size_x, size_y,
    ids_hbm, owner_hbm, feat_hbm, conv_hbm, bias_hbm, down_hbm,
    out_ref,
    ids, owner, feat, conv, bias, down,
    index, face_send, edge_send, face_recv, edge_recv, table, ytab, etab,
    stack, outer, lines, columns, acc, band, down_both, place, spread, stage,
    load_sem, halo_send, halo_recv, out_send, out_recv, own_sem, known_sem,
):
    i = lax.axis_index("bx")
    j = lax.axis_index("by")
    z, y = j // SIDE, lax.rem(j, SIDE)

    loads = [
        pltpu.make_async_copy(source, target, load_sem.at[k])
        for k, (source, target) in enumerate(
            [
                (feat_hbm, feat),
                (conv_hbm, conv),
                (ids_hbm, ids),
                (owner_hbm, owner),
                (bias_hbm, bias),
                (down_hbm, down),
            ]
        )
    ]
    for load in loads:
        load.start()

    def inside(step_x, step_y):
        x_in = (i + step_x >= 0) & (i + step_x < size_x)
        return x_in & (j + step_y >= 0) & (j + step_y < size_y)

    def partner(step_z, step_y):
        return lax.rem(z + step_z, SIDE) * SIDE + lax.rem(y + step_y, SIDE)

    straight = [(0, 1), (0, 3), (1, 0), (3, 0), (0, 2), (2, 0)]
    turning = [(1, 1), (3, 3), (1, 2), (3, 2), (2, 2), (2, 1), (2, 3), (1, 3), (3, 1)]

    barrier = pltpu.get_barrier_semaphore()
    greetings = j
    for step_x, step_y in HALO:
        here = inside(step_x, step_y)
        greetings = greetings + jnp.where(here, 1, 0)

        @pl.when(here)
        def _(step_x=step_x, step_y=step_y):
            pl.semaphore_signal(
                barrier, inc=1, device_id=(i + step_x, j + step_y), device_id_type=MESH
            )

    for d in range(1, size_y):

        @pl.when(j + d < size_y)
        def _(d=d):
            pl.semaphore_signal(barrier, inc=1, device_id=(i, j + d), device_id_type=MESH)

    pick = picked_rows()
    loads[0].wait()
    picked = jnp.dot(pick, feat[...], preferred_element_type=F32)
    for k in range(4):
        face_send[k] = picked[k * FACE : (k + 1) * FACE].astype(BF16)
        first = 4 * FACE + k * BRICKS
        edge = picked[first : first + BRICKS]
        edge_send[k] = jnp.concatenate([edge[:, 0:256], edge[:, 256:512]], 0).astype(BF16)

    pl.semaphore_wait(barrier, greetings)
    copies = []
    for k, (step_x, step_y) in enumerate(HALO):
        if k < 4:
            source, target = face_send.at[k], face_recv.at[k]
        else:
            source, target = edge_send.at[k - 4], edge_recv.at[k - 4]
        copy = pltpu.make_async_remote_copy(
            src_ref=source,
            dst_ref=target,
            send_sem=halo_send.at[k],
            recv_sem=halo_recv.at[k],
            device_id=(i + step_x, j + step_y),
            device_id_type=MESH,
        )
        copies.append((copy, inside(step_x, step_y), inside(-step_x, -step_y)))
    for copy, sent, received in copies[2:4] + copies[4::3] + copies[5:7] + copies[:2]:
        pl.when(sent)(copy.start)

    for d in range(1, size_y):

        @pl.when(j >= d)
        def _(d=d):
            pl.semaphore_signal(known_sem, inc=1, device_id=(i, j - d), device_id_type=MESH)

    table[0:T_FACE] = feat[...].astype(F32).reshape(T_FACE, EDGE, LANES)
    table[T_ZERO:T_SIZE] = jnp.zeros((EDGE, EDGE, LANES), F32)
    loads[2].wait()

    def locate(bricks, taps):
        for g in bricks:
            for tap in taps:
                sx, sy = tap // 9 - 1, tap // 3 % 3 - 1
                value = ids[g, tap]
                brick = value & 7
                far_x = jnp.where(value >> 3 >> 4 == i, 0, 1)
                far_y = jnp.where((value >> 3) & 15 == j, 0, 1)
                if sx == 0 and sy == 0:
                    row, zero = brick * EDGE, T_ZERO
                elif sy == 0:
                    edge_x, side = (7, 0) if sx < 0 else (0, 1)
                    row = jnp.where(
                        far_x == 0, brick * EDGE + edge_x, T_FACE + side * BRICKS + brick
                    )
                    zero = T_ZERO
                elif sx == 0:
                    row, zero = far_y * BRICKS + brick, Y_ZERO
                else:
                    row, zero = far_x * 16 + far_y * 8 + brick, E_ZERO
                index[g, tap] = jnp.where(value >= 0, row, zero)

    locate(range(BRICKS), (12, 14))

    loads[1].wait()
    empty = jnp.zeros((CH, CH), BF16)
    blank = jnp.zeros((CH, 2 * CH), BF16)
    for ty in range(3):
        for tx in range(3):
            w = [conv[tx * 9 + ty * 3 + tz] * jnp.array(0.5, BF16) for tz in range(3)]
            pairs = {
                -1: jnp.concatenate([w[0], empty], 1),
                0: jnp.concatenate([w[1], w[0]], 1),
                1: jnp.concatenate([w[2], w[1]], 1),
                2: jnp.concatenate([empty, w[2]], 1),
            }
            for place_in, depth_in in enumerate((0, 1, 2, 3, 4, -1)):
                for q in range(2):
                    first = tx * BAND + place_in * CH
                    band[ty, first : first + CH, q * 128 : (q + 1) * 128] = pairs.get(
                        depth_in - 2 * q, blank
                    )
    loads[5].wait()
    for a in range(2):
        for b in range(2):
            for k in range(2):
                first = (a * 2 + k) * CH
                down_both[first : first + CH, b * CO : (b + 1) * CO] = down[a * 4 + b * 2 + k]

    low = iota((EDGE, 128), 1) < CH

    def halves(c, m, p):
        e0 = jnp.where(low, c[:, 256:384], m)
        e1 = jnp.where(low, p, c[:, 128:256])
        return (
            jnp.concatenate([c[:, 0:256], e0], 1),
            jnp.concatenate([c[:, 256:512], e1], 1),
        )

    def local_slab(g, x):
        return halves(
            table[g * EDGE + x],
            table[index[g, 12] + x, :, LANES - 128 : LANES],
            table[index[g, 14] + x, :, 0:128],
        )

    stack[0] = jnp.zeros((2, FACE, BAND), BF16)
    stack[9] = jnp.zeros((2, FACE, BAND), BF16)
    for k in range(2):
        columns[k, 0] = jnp.zeros((16, BAND), BF16)
        columns[k, 9] = jnp.zeros((16, BAND), BF16)

    def gather_local(slabs):
        for x in slabs:
            for pair in range(BRICKS // 2):
                even, odd = local_slab(pair * 2, x), local_slab(pair * 2 + 1, x)
                for h in range(2):
                    both = jnp.concatenate([even[h], odd[h]], 0)
                    stack[x + 1, h, pair * 16 : pair * 16 + 16] = both.astype(BF16)

    def windows(source, first, count, rows):
        return jnp.concatenate(
            [source[first + tx : first + tx + count].reshape(rows, BAND) for tx in range(3)], 1
        )

    def shifted(part, ty):
        if ty == 1:
            return part
        moved = pltpu.roll(part.reshape(-1, 8, HALF), 1 if ty == 0 else 7, 1)
        return moved.reshape(part.shape)

    def convolve_local(first, count):
        rows = count * 2 * FACE
        window = windows(stack, first, count, rows)
        y_of = iota((rows, HALF), 0) & 7
        total = jnp.dot(window, band[1], preferred_element_type=F32)
        for ty, empty in ((0, 0), (2, 7)):
            part = jnp.dot(window, band[ty], preferred_element_type=F32)
            total = total + jnp.where(y_of == empty, 0.0, shifted(part, ty))
        acc[first : first + count] = total.reshape(count, 2, FACE, HALF)

    rest = [tap for tap in range(27) if tap not in (12, 13, 14)]
    gather_local(range(0, 5))
    convolve_local(0, 4)
    locate(range(0, 4), rest)
    gather_local(range(5, 8))
    convolve_local(4, 4)
    locate(range(4, 8), rest)

    for k in range(2):
        ytab[k, 0:BRICKS] = picked[(2 + k) * FACE : (3 + k) * FACE].reshape(BRICKS, EDGE, LANES)
        ytab[k, Y_ZERO] = jnp.zeros((EDGE, LANES), F32)
    for k in range(4):
        repeat_rows(etab, k, 0, picked, 4 * FACE + k * BRICKS)
        etab[k, E_ZERO] = jnp.zeros((EDGE, LANES), F32)

    loads[3].wait()
    owners = [owner[0, g] for g in range(BRICKS)]
    row, col = iota((8 * CHUNK, FACE * CHUNK), 0), iota((8 * CHUNK, FACE * CHUNK), 1)
    slot_of = jnp.zeros((8 * CHUNK, FACE * CHUNK), jnp.int32)
    for g in range(BRICKS):
        rank = jnp.int32(0)
        for earlier in range(g):
            rank = rank + jnp.where(owners[earlier] == owners[g], 1, 0)
        slot_of = jnp.where((col >> 3) & 7 == g, owners[g] * 2 + rank, slot_of)
    slot_of = jnp.where((col >> 6 == row >> 3) & (col & 7 == (row & 7) * 2), slot_of, -1)
    blocks = [(slot_of == s).astype(F32) for s in range(2 * size_y)]
    place[...] = jnp.concatenate(blocks, 0).astype(BF16)

    row, col = iota((128, 128), 0), iota((128, 128), 1)
    turned = ((row >> 3) & 1) * 64 + (row & 7) * 8 + (row >> 4) == col
    turned = turned.astype(F32).astype(BF16)
    count = 2 * CHUNK * 16
    row, col = iota((count * 8, count * 4), 0), iota((count * 8, count * 4), 1)
    wanted = (col // (2 * count)) * 7
    spread[...] = (
        ((row >> 3 == lax.rem(col, count)) & (row & 7 == wanted)).astype(F32).astype(BF16)
    )

    loads[4].wait()

    def arrive(some):
        for copy, sent, received in some:
            pl.when(sent)(copy.wait_send)
            pl.when(received)(copy.wait_recv)

    arrive(copies[2:4])
    over_y = [face_recv[2 + k].astype(F32) for k in range(2)]
    for k in range(2):
        ytab[k, BRICKS : 2 * BRICKS] = over_y[k].reshape(BRICKS, EDGE, LANES)

    def line(g, side):
        tap = 9 + side * 6
        return halves(
            ytab[side, index[g, tap + 1]],
            ytab[side, index[g, tap], :, LANES - 128 : LANES],
            ytab[side, index[g, tap + 2], :, 0:128],
        )

    for side in range(2):
        for pair in range(BRICKS // 2):
            even, odd = line(pair * 2, side), line(pair * 2 + 1, side)
            for h in range(2):
                first = h * FACE + pair * 16
                both = jnp.concatenate([even[h], odd[h]], 0)
                lines[side, first : first + 16] = both.astype(BF16)
    for side in range(2):
        moved = jnp.dot(turned, lines[side], preferred_element_type=F32)
        columns[side, 1:9] = moved.astype(BF16).reshape(8, 16, BAND)
    terms = []
    for side in range(2):
        window = windows(columns.at[side], 0, 8, 128)
        value = jnp.dot(window, band[side * 2], preferred_element_type=F32)
        high = value.astype(BF16)
        terms.append((high, (value - high.astype(F32)).astype(BF16)))
    def order(chunk):
        return ORDER[chunk * CHUNK : chunk * CHUNK + CHUNK]

    def convolved(chunk):
        part = jnp.concatenate(
            [term[32 * k : 32 * k + 32] for pair in terms for term in pair for k in order(chunk)],
            0,
        )
        total = jnp.concatenate([acc[2 * k : 2 * k + 2] for k in order(chunk)], 0)
        return total.reshape(size, HALF) + jnp.dot(spread[...], part, preferred_element_type=F32)

    slabs = 2 * CHUNK
    size = slabs * 2 * FACE

    def out_copy(chunk, steps):
        dest = partner(*steps)
        return pltpu.make_async_remote_copy(
            src_ref=stage.at[chunk, pl.ds(dest * 2, 2)],
            dst_ref=out_ref.at[pl.ds(j * 2, 2), pl.ds(chunk * CHUNK, CHUNK)],
            send_sem=out_send.at[chunk, steps[0] * SIDE + steps[1]],
            recv_sem=out_recv.at[chunk, steps[0] * SIDE + steps[1]],
            device_id=(i, dest),
            device_id_type=MESH,
        )

    def own_copy(chunk):
        return pltpu.make_async_copy(
            stage.at[chunk, pl.ds(j * 2, 2)],
            out_ref.at[pl.ds(j * 2, 2), pl.ds(chunk * CHUNK, CHUNK)],
            own_sem.at[chunk],
        )

    bias_row = jnp.concatenate([bias[...] * 0.5] * 4, 1)
    def reduced(chunk, total):
        half_v = total + bias_row
        own = jnp.concatenate(
            [stack[2 * k + 1 : 2 * k + 3, :, :, 0:HALF] for k in order(chunk)], 0
        ).reshape(size, HALF)
        hidden = own.astype(F32) + (half_v + half_v * jnp.tanh(half_v))
        hidden = hidden.astype(BF16).reshape(CHUNK, 2, 2 * FACE, HALF)
        lhs = jnp.concatenate(
            [
                jnp.concatenate([hidden[:, a, :, k * 128 : (k + 1) * 128] for a in range(2)], 2)
                for k in range(2)
            ],
            0,
        ).reshape(2 * CHUNK * 2 * FACE, 256)
        coarse = jnp.dot(lhs, down_both[...], preferred_element_type=F32)
        odd = pltpu.roll(coarse[:, CO:].reshape(-1, 8, CO), 7, 1).reshape(-1, CO)
        coarse = (coarse[:, :CO] + odd).astype(BF16).reshape(2, CHUNK, 2, FACE, CO)
        return jnp.concatenate(
            [coarse[k, :, h] for h in range(2) for k in range(2)], 2
        ).reshape(CHUNK * FACE, 4 * CO)

    def staged(chunk, coarse):
        placed = jnp.dot(place[...], coarse, preferred_element_type=F32)
        placed = placed.reshape(2 * size_y, CHUNK, 8, 4 * CO)[:, :, 0:4]
        stage[chunk] = placed.astype(BF16)

    def send(chunk):
        if chunk == 0:

            @pl.when(j + 1 < size_y)
            def _():
                pl.semaphore_wait(known_sem, size_y - 1 - j)

        for steps in turning + straight:
            out_copy(chunk, steps).start()
        own_copy(chunk).start()

    staged(0, reduced(0, convolved(0)))
    send(0)

    arrive(copies[:2] + copies[4:])
    for k in range(2):
        over_x = face_recv[k].astype(F32)
        first = T_FACE + k * BRICKS
        table[first : first + BRICKS] = over_x.reshape(BRICKS, EDGE, LANES)
        for side in range(2):
            at = 0 if side else 7
            repeat_rows(etab, side * 2 + k, 8, over_y[k], at, EDGE)
            repeat_rows(etab, k * 2 + side, 16, over_x, at, EDGE)
            edge = edge_recv[k * 2 + side].astype(F32)
            edge = jnp.concatenate([edge[0:8], edge[8:16]], 1)
            repeat_rows(etab, k * 2 + side, 24, edge)

    last_row = iota((EDGE, BAND), 0) == 7
    first_row = iota((EDGE, BAND), 0) == 0

    def outer_slab(g, side):
        sx = side * 2 - 1
        result = []
        for sy in STEPS:
            tap = (sx + 1) * 9 + (sy + 1) * 3
            source = table if sy == 0 else etab.at[side * 2 + (sy + 1) // 2]
            result.append(
                halves(
                    source[index[g, tap + 1]],
                    source[index[g, tap], :, LANES - 128 : LANES],
                    source[index[g, tap + 2], :, 0:128],
                )
            )
        before, same, after = result
        return [
            [
                jnp.where(last_row, before[h], same[h]),
                same[h],
                jnp.where(first_row, after[h], same[h]),
            ]
            for h in range(2)
        ]

    for side in range(2):
        for pair in range(BRICKS // 2):
            even, odd = outer_slab(pair * 2, side), outer_slab(pair * 2 + 1, side)
            for h in range(2):
                for ty in range(3):
                    both = jnp.concatenate([even[h][ty], odd[h][ty]], 0)
                    outer[side, ty, h, pair * 16 : pair * 16 + 16] = both.astype(BF16)
    for side in range(2):
        extra = None
        for ty in range(3):
            first = side * 2 * BAND
            part = jnp.dot(
                outer[side, ty].reshape(2 * FACE, BAND),
                band[ty, first : first + BAND],
                preferred_element_type=F32,
            )
            part = shifted(part, ty)
            extra = part if extra is None else extra + part
        acc[side * 7] = acc[side * 7] + extra.reshape(2, FACE, HALF)

    staged(1, reduced(1, convolved(1)))
    send(1)
    for chunk in range(CHUNKS):
        for steps in straight + turning:
            out_copy(chunk, steps).wait()
        own_copy(chunk).wait()


def hand_over(source, target, held, in_sem, out_sem):
    ins, outs = [], []
    for k, x in enumerate(ORDER):
        ins.append(pltpu.make_async_copy(source.at[:, k], held.at[k], in_sem.at[k]))
        outs.append(pltpu.make_async_copy(held.at[k], target.at[:, x], out_sem.at[k]))
    for copy in ins:
        copy.start()
    for arrived, leaving in zip(ins, outs):
        arrived.wait()
        leaving.start()
    for copy in outs:
        copy.wait()


def shards(features, neighbour_ids, conv_weight, conv_bias, down_weight, coarse_owner):
    size_x = lax.axis_size("bx")
    size_y = lax.axis_size("by")
    slots = 2 * size_y
    hbm_spec = pl.BlockSpec(memory_space=pltpu.HBM)
    out = pl.pallas_call(
        functools.partial(kernel, size_x, size_y),
        out_shape=jax.ShapeDtypeStruct((slots, 4, 4, 4 * CO), BF16),
        in_specs=[hbm_spec] * 6,
        out_specs=pl.BlockSpec(memory_space=pl.ANY),
        scratch_shapes=[
            pltpu.SMEM((BRICKS, 27), jnp.int32),
            pltpu.SMEM((1, BRICKS), jnp.int32),
            pltpu.VMEM((ROWS, LANES), BF16),
            pltpu.VMEM((27, CH, CH), BF16),
            pltpu.VMEM((1, CH), F32),
            pltpu.VMEM((8, CH, CO), BF16),
            pltpu.SMEM((BRICKS, 27), jnp.int32),
            pltpu.VMEM((4, FACE, LANES), BF16),
            pltpu.VMEM((4, 16, 256), BF16),
            pltpu.VMEM((4, FACE, LANES), BF16),
            pltpu.VMEM((4, 16, 256), BF16),
            pltpu.VMEM((T_SIZE, EDGE, LANES), F32),
            pltpu.VMEM((2, Y_SIZE, EDGE, LANES), F32),
            pltpu.VMEM((4, E_SIZE, EDGE, LANES), F32),
            pltpu.VMEM((10, 2, FACE, BAND), BF16),
            pltpu.VMEM((2, 3, 2, FACE, BAND), BF16),
            pltpu.VMEM((2, 2 * FACE, BAND), BF16),
            pltpu.VMEM((2, 10, 16, BAND), BF16),
            pltpu.VMEM((EDGE, 2, FACE, HALF), F32),
            pltpu.VMEM((3, 3 * BAND, HALF), BF16),
            pltpu.VMEM((256, 2 * CO), BF16),
            pltpu.VMEM((slots * 8 * CHUNK, FACE * CHUNK), BF16),
            pltpu.VMEM((256 * CHUNK, 128 * CHUNK), BF16),
            pltpu.VMEM((CHUNKS, slots, CHUNK, 4, 4 * CO), BF16),
            pltpu.SemaphoreType.DMA((6,)),
            pltpu.SemaphoreType.DMA((8,)),
            pltpu.SemaphoreType.DMA((8,)),
            pltpu.SemaphoreType.DMA((CHUNKS, size_y)),
            pltpu.SemaphoreType.DMA((CHUNKS, size_y)),
            pltpu.SemaphoreType.DMA((CHUNKS,)),
            pltpu.SemaphoreType.REGULAR,
        ],
        compiler_params=pltpu.CompilerParams(
            collective_id=0, has_side_effects=True, vmem_limit_bytes=63 * 1024 * 1024
        ),
        name="brick_encoder",
    )(
        neighbour_ids,
        coarse_owner.reshape(1, BRICKS),
        features.reshape(ROWS, LANES),
        conv_weight,
        conv_bias.reshape(1, CH),
        down_weight,
    )
    return pl.pallas_call(
        hand_over,
        out_shape=jax.ShapeDtypeStruct(out.shape, out.dtype),
        in_specs=[pl.BlockSpec(memory_space=pl.ANY)],
        out_specs=pl.BlockSpec(memory_space=pl.ANY),
        scratch_shapes=[
            pltpu.VMEM((4, slots, 4, 4 * CO), out.dtype),
            pltpu.SemaphoreType.DMA((4,)),
            pltpu.SemaphoreType.DMA((4,)),
        ],
        compiler_params=pltpu.CompilerParams(vmem_limit_bytes=63 * 1024 * 1024),
        name="hand_over",
    )(out)


def solution(mesh):
    in_specs = (
        P(("bx", "by"), None, None, None),
        P(("bx", "by"), None),
        P(),
        P(),
        P(),
        P(("bx", "by"), None),
    )
    out_specs = P(("bx", "by"), None, None, None)
    return jax.shard_map(shards, mesh=mesh, in_specs=in_specs, out_specs=out_specs, check_vma=False)
```

```python
import functools

import jax
import jax.numpy as jnp
from jax import lax
from jax.experimental import pallas as pl
from jax.experimental.pallas import tpu as pltpu
from jax.sharding import PartitionSpec as P

MESH = pl.DeviceIdType.MESH
F32 = jnp.float32
BF16 = jnp.bfloat16

EDGE = 8
BRICKS = 8
CH = 64
CO = 128
LANES = EDGE * CH
ROWS = BRICKS * EDGE * EDGE
HALF = 4 * CH
BAND = 6 * CH
FACE = BRICKS * EDGE

T_FACE = BRICKS * EDGE
T_ZERO = T_FACE + 2 * BRICKS
T_SIZE = T_ZERO + EDGE
Y_ZERO = 2 * BRICKS
Y_SIZE = Y_ZERO + 1
E_ZERO = 4 * BRICKS
E_SIZE = E_ZERO + 1

STEPS = (-1, 0, 1)
CHUNK = 2
CHUNKS = EDGE // 2 // CHUNK
ORDER = (1, 2, 0, 3)
SIDE = 4
HALO = [(1, 0), (-1, 0), (0, 1), (0, -1), (1, 1), (1, -1), (-1, 1), (-1, -1)]


def iota(shape, dim):
    return lax.broadcasted_iota(jnp.int32, shape, dim)


def picked_rows():
    targets = []
    inner = iota((FACE, 128), 0)
    for first in (56, 0):
        targets.append((inner >> 3) * 64 + first + (inner & 7))
    for first in (7, 0):
        targets.append(inner * 8 + first)
    inner = iota((4 * BRICKS, 128), 0)
    corner = inner >> 3
    targets.append(
        (inner & 7) * 64 + jnp.where(corner < 2, 56, 0) + jnp.where(corner & 1 == 0, 7, 0)
    )
    target = jnp.concatenate(targets, 0)
    target = target - iota(target.shape, 1)
    blocks = [(target == 128 * k).astype(F32) for k in range(ROWS // 128)]
    return jnp.concatenate(blocks, 1).astype(BF16)


def repeat_rows(target, corner, first, rows, start=0, step=1):
    for k in range(BRICKS):
        row = start + step * k
        target[corner, first + k] = jnp.broadcast_to(rows[row : row + 1], (EDGE, LANES))


def kernel(
    size_x, size_y,
    ids_hbm, owner_hbm, feat_hbm, conv_hbm, bias_hbm, down_hbm,
    out_ref,
    ids, owner, feat, conv, bias, down,
    located, index, face_send, edge_send, face_recv, edge_recv, table, ytab, etab,
    stack, outer, lines, columns, acc, band, down_both, place, spread, stage,
    load_sem, locate_sem, halo_send, halo_recv, out_send, out_recv, own_sem, known_sem,
):
    i = lax.axis_index("bx")
    j = lax.axis_index("by")
    z, y = j // SIDE, lax.rem(j, SIDE)

    loads = [
        pltpu.make_async_copy(source, target, load_sem.at[k])
        for k, (source, target) in enumerate(
            [
                (feat_hbm, feat),
                (conv_hbm, conv),
                (ids_hbm, ids),
                (owner_hbm, owner),
                (bias_hbm, bias),
                (down_hbm, down),
            ]
        )
    ]
    for load in loads:
        load.start()

    def inside(step_x, step_y):
        x_in = (i + step_x >= 0) & (i + step_x < size_x)
        return x_in & (j + step_y >= 0) & (j + step_y < size_y)

    def partner(step_z, step_y):
        return lax.rem(z + step_z, SIDE) * SIDE + lax.rem(y + step_y, SIDE)

    straight = [(0, 1), (0, 3), (1, 0), (3, 0), (0, 2), (2, 0)]
    turning = [(1, 1), (3, 3), (1, 2), (3, 2), (2, 2), (2, 1), (2, 3), (1, 3), (3, 1)]

    barrier = pltpu.get_barrier_semaphore()
    greetings = j
    for step_x, step_y in HALO:
        here = inside(step_x, step_y)
        greetings = greetings + jnp.where(here, 1, 0)

        @pl.when(here)
        def _(step_x=step_x, step_y=step_y):
            pl.semaphore_signal(
                barrier, inc=1, device_id=(i + step_x, j + step_y), device_id_type=MESH
            )

    for d in range(1, size_y):

        @pl.when(j + d < size_y)
        def _(d=d):
            pl.semaphore_signal(barrier, inc=1, device_id=(i, j + d), device_id_type=MESH)

    pick = picked_rows()
    loads[0].wait()
    picked = jnp.dot(pick, feat[...], preferred_element_type=F32)
    for k in range(4):
        face_send[k] = picked[k * FACE : (k + 1) * FACE].astype(BF16)
        first = 4 * FACE + k * BRICKS
        edge = picked[first : first + BRICKS]
        edge_send[k] = jnp.concatenate([edge[:, 0:256], edge[:, 256:512]], 0).astype(BF16)

    loads[2].wait()
    value, tap = ids[...], iota((BRICKS, 27), 1)
    sx = jnp.where(tap < 9, -1, jnp.where(tap < 18, 0, 1))
    inner = tap - 9 * (sx + 1)
    sy = jnp.where(inner < 3, -1, jnp.where(inner < 6, 0, 1))
    brick = value & 7
    far_x = jnp.where((value >> 7) == i, 0, 1)
    far_y = jnp.where(((value >> 3) & 15) == j, 0, 1)
    near = brick * EDGE + jnp.where(sx < 0, 7, 0)
    far = T_FACE + jnp.where(sx < 0, 0, BRICKS) + brick
    flat = jnp.where(sx == 0, brick * EDGE, jnp.where(far_x == 0, near, far))
    bent = jnp.where(sx == 0, 0, far_x * 16) + far_y * 8 + brick
    nothing = jnp.where(sx == 0, Y_ZERO, E_ZERO)
    located[...] = jnp.where(
        value >= 0, jnp.where(sy == 0, flat, bent), jnp.where(sy == 0, T_ZERO, nothing)
    )
    locating = pltpu.make_async_copy(located, index, locate_sem)
    locating.start()

    pl.semaphore_wait(barrier, greetings)
    copies = []
    for k, (step_x, step_y) in enumerate(HALO):
        if k < 4:
            source, target = face_send.at[k], face_recv.at[k]
        else:
            source, target = edge_send.at[k - 4], edge_recv.at[k - 4]
        copy = pltpu.make_async_remote_copy(
            src_ref=source,
            dst_ref=target,
            send_sem=halo_send.at[k],
            recv_sem=halo_recv.at[k],
            device_id=(i + step_x, j + step_y),
            device_id_type=MESH,
        )
        copies.append((copy, inside(step_x, step_y), inside(-step_x, -step_y)))
    for copy, sent, received in copies[2:4] + copies[4::3] + copies[5:7] + copies[:2]:
        pl.when(sent)(copy.start)

    for d in range(1, size_y):

        @pl.when(j >= d)
        def _(d=d):
            pl.semaphore_signal(known_sem, inc=1, device_id=(i, j - d), device_id_type=MESH)

    table[0:T_FACE] = feat[...].astype(F32).reshape(T_FACE, EDGE, LANES)
    table[T_ZERO:T_SIZE] = jnp.zeros((EDGE, EDGE, LANES), F32)
    loads[1].wait()
    empty = jnp.zeros((CH, CH), BF16)
    blank = jnp.zeros((CH, 2 * CH), BF16)
    for ty in range(3):
        for tx in range(3):
            w = [conv[tx * 9 + ty * 3 + tz] * jnp.array(0.5, BF16) for tz in range(3)]
            pairs = {
                -1: jnp.concatenate([w[0], empty], 1),
                0: jnp.concatenate([w[1], w[0]], 1),
                1: jnp.concatenate([w[2], w[1]], 1),
                2: jnp.concatenate([empty, w[2]], 1),
            }
            for place_in, depth_in in enumerate((0, 1, 2, 3, 4, -1)):
                for q in range(2):
                    first = tx * BAND + place_in * CH
                    band[ty, first : first + CH, q * 128 : (q + 1) * 128] = pairs.get(
                        depth_in - 2 * q, blank
                    )
    loads[5].wait()
    for a in range(2):
        for b in range(2):
            for k in range(2):
                first = (a * 2 + k) * CH
                down_both[first : first + CH, b * CO : (b + 1) * CO] = down[a * 4 + b * 2 + k]

    low = iota((EDGE, 128), 1) < CH

    def halves(c, m, p):
        e0 = jnp.where(low, c[:, 256:384], m)
        e1 = jnp.where(low, p, c[:, 128:256])
        return (
            jnp.concatenate([c[:, 0:256], e0], 1),
            jnp.concatenate([c[:, 256:512], e1], 1),
        )

    def local_slab(g, x):
        return halves(
            table[g * EDGE + x],
            table[index[g, 12] + x, :, LANES - 128 : LANES],
            table[index[g, 14] + x, :, 0:128],
        )

    stack[0] = jnp.zeros((2, FACE, BAND), BF16)
    stack[9] = jnp.zeros((2, FACE, BAND), BF16)
    for k in range(2):
        columns[k, 0] = jnp.zeros((16, BAND), BF16)
        columns[k, 9] = jnp.zeros((16, BAND), BF16)

    def gather_local(slabs):
        for x in slabs:
            for pair in range(BRICKS // 2):
                even, odd = local_slab(pair * 2, x), local_slab(pair * 2 + 1, x)
                for h in range(2):
                    both = jnp.concatenate([even[h], odd[h]], 0)
                    stack[x + 1, h, pair * 16 : pair * 16 + 16] = both.astype(BF16)

    def windows(source, first, count, rows):
        return jnp.concatenate(
            [source[first + tx : first + tx + count].reshape(rows, BAND) for tx in range(3)], 1
        )

    def shifted(part, ty):
        if ty == 1:
            return part
        moved = pltpu.roll(part.reshape(-1, 8, HALF), 1 if ty == 0 else 7, 1)
        return moved.reshape(part.shape)

    def convolve_local(first, count):
        rows = count * 2 * FACE
        window = windows(stack, first, count, rows)
        y_of = iota((rows, HALF), 0) & 7
        total = jnp.dot(window, band[1], preferred_element_type=F32)
        for ty, empty in ((0, 0), (2, 7)):
            part = jnp.dot(window, band[ty], preferred_element_type=F32)
            total = total + jnp.where(y_of == empty, 0.0, shifted(part, ty))
        acc[first : first + count] = total.reshape(count, 2, FACE, HALF)

    locating.wait()
    gather_local(range(0, 5))
    convolve_local(0, 4)
    gather_local(range(5, 8))
    convolve_local(4, 4)

    for k in range(2):
        ytab[k, 0:BRICKS] = picked[(2 + k) * FACE : (3 + k) * FACE].reshape(BRICKS, EDGE, LANES)
        ytab[k, Y_ZERO] = jnp.zeros((EDGE, LANES), F32)
    for k in range(4):
        repeat_rows(etab, k, 0, picked, 4 * FACE + k * BRICKS)
        etab[k, E_ZERO] = jnp.zeros((EDGE, LANES), F32)

    loads[3].wait()
    owners = [owner[0, g] for g in range(BRICKS)]
    row, col = iota((4 * CHUNK, FACE * CHUNK), 0), iota((4 * CHUNK, FACE * CHUNK), 1)
    slot_of = jnp.zeros((4 * CHUNK, FACE * CHUNK), jnp.int32)
    for g in range(BRICKS):
        rank = jnp.int32(0)
        for earlier in range(g):
            rank = rank + jnp.where(owners[earlier] == owners[g], 1, 0)
        slot_of = jnp.where((col >> 3) & 7 == g, owners[g] * 2 + rank, slot_of)
    slot_of = jnp.where((col >> 6 == row >> 2) & (col & 7 == (row & 3) * 2), slot_of, -1)
    blocks = [(slot_of == s).astype(F32) for s in range(2 * size_y)]
    place[...] = jnp.concatenate(blocks, 0).astype(BF16)

    row, col = iota((128, 128), 0), iota((128, 128), 1)
    turned = ((row >> 3) & 1) * 64 + (row & 7) * 8 + (row >> 4) == col
    turned = turned.astype(F32).astype(BF16)
    count = 2 * CHUNK * 16
    row, col = iota((count * 8, count * 4), 0), iota((count * 8, count * 4), 1)
    wanted = (col // (2 * count)) * 7
    spread[...] = (
        ((row >> 3 == lax.rem(col, count)) & (row & 7 == wanted)).astype(F32).astype(BF16)
    )

    loads[4].wait()

    def arrive(some):
        for copy, sent, received in some:
            pl.when(sent)(copy.wait_send)
            pl.when(received)(copy.wait_recv)

    arrive(copies[2:4])
    over_y = [face_recv[2 + k].astype(F32) for k in range(2)]
    for k in range(2):
        ytab[k, BRICKS : 2 * BRICKS] = over_y[k].reshape(BRICKS, EDGE, LANES)

    def line(g, side):
        tap = 9 + side * 6
        return halves(
            ytab[side, index[g, tap + 1]],
            ytab[side, index[g, tap], :, LANES - 128 : LANES],
            ytab[side, index[g, tap + 2], :, 0:128],
        )

    for side in range(2):
        for pair in range(BRICKS // 2):
            even, odd = line(pair * 2, side), line(pair * 2 + 1, side)
            for h in range(2):
                first = h * FACE + pair * 16
                both = jnp.concatenate([even[h], odd[h]], 0)
                lines[side, first : first + 16] = both.astype(BF16)
    for side in range(2):
        moved = jnp.dot(turned, lines[side], preferred_element_type=F32)
        columns[side, 1:9] = moved.astype(BF16).reshape(8, 16, BAND)
    terms = []
    for side in range(2):
        window = windows(columns.at[side], 0, 8, 128)
        value = jnp.dot(window, band[side * 2], preferred_element_type=F32)
        high = value.astype(BF16)
        terms.append((high, (value - high.astype(F32)).astype(BF16)))
    def order(chunk):
        return ORDER[chunk * CHUNK : chunk * CHUNK + CHUNK]

    def convolved(chunk):
        part = jnp.concatenate(
            [term[32 * k : 32 * k + 32] for pair in terms for term in pair for k in order(chunk)],
            0,
        )
        total = jnp.concatenate([acc[2 * k : 2 * k + 2] for k in order(chunk)], 0)
        return total.reshape(size, HALF) + jnp.dot(spread[...], part, preferred_element_type=F32)

    slabs = 2 * CHUNK
    size = slabs * 2 * FACE

    def out_copy(chunk, steps):
        dest = partner(*steps)
        return pltpu.make_async_remote_copy(
            src_ref=stage.at[chunk, pl.ds(dest * 2, 2)],
            dst_ref=out_ref.at[pl.ds(j * 2, 2), pl.ds(chunk * CHUNK, CHUNK)],
            send_sem=out_send.at[chunk, steps[0] * SIDE + steps[1]],
            recv_sem=out_recv.at[chunk, steps[0] * SIDE + steps[1]],
            device_id=(i, dest),
            device_id_type=MESH,
        )

    def own_copy(chunk):
        return pltpu.make_async_copy(
            stage.at[chunk, pl.ds(j * 2, 2)],
            out_ref.at[pl.ds(j * 2, 2), pl.ds(chunk * CHUNK, CHUNK)],
            own_sem.at[chunk],
        )

    bias_row = jnp.concatenate([bias[...] * 0.5] * 4, 1)
    def reduced(chunk, total):
        half_v = total + bias_row
        own = jnp.concatenate(
            [stack[2 * k + 1 : 2 * k + 3, :, :, 0:HALF] for k in order(chunk)], 0
        ).reshape(size, HALF)
        hidden = own.astype(F32) + (half_v + half_v * jnp.tanh(half_v))
        hidden = hidden.astype(BF16).reshape(CHUNK, 2, 2 * FACE, HALF)
        lhs = jnp.concatenate(
            [
                jnp.concatenate([hidden[:, a, :, k * 128 : (k + 1) * 128] for a in range(2)], 2)
                for k in range(2)
            ],
            0,
        ).reshape(2 * CHUNK * 2 * FACE, 256)
        coarse = jnp.dot(lhs, down_both[...], preferred_element_type=F32)
        odd = pltpu.roll(coarse[:, CO:].reshape(-1, 8, CO), 7, 1).reshape(-1, CO)
        coarse = (coarse[:, :CO] + odd).astype(BF16).reshape(2, CHUNK, 2, FACE, CO)
        return jnp.concatenate(
            [coarse[k, :, h] for h in range(2) for k in range(2)], 2
        ).reshape(CHUNK * FACE, 4 * CO)

    def staged(chunk, coarse):
        placed = jnp.dot(place[...], coarse, preferred_element_type=F32)
        placed = placed.reshape(2 * size_y, 4 * CHUNK, 4 * CO)
        for k in range(CHUNK):
            stage[chunk, :, k] = placed[:, 4 * k : 4 * k + 4].astype(BF16)

    def send(chunk):
        if chunk == 0:

            @pl.when(j + 1 < size_y)
            def _():
                pl.semaphore_wait(known_sem, size_y - 1 - j)

        for steps in turning + straight:
            out_copy(chunk, steps).start()
        own_copy(chunk).start()

    staged(0, reduced(0, convolved(0)))
    send(0)

    arrive(copies[:2] + copies[4:])
    for k in range(2):
        over_x = face_recv[k].astype(F32)
        first = T_FACE + k * BRICKS
        table[first : first + BRICKS] = over_x.reshape(BRICKS, EDGE, LANES)
        for side in range(2):
            at = 0 if side else 7
            repeat_rows(etab, side * 2 + k, 8, over_y[k], at, EDGE)
            repeat_rows(etab, k * 2 + side, 16, over_x, at, EDGE)
            edge = edge_recv[k * 2 + side].astype(F32)
            edge = jnp.concatenate([edge[0:8], edge[8:16]], 1)
            repeat_rows(etab, k * 2 + side, 24, edge)

    last_row = iota((EDGE, BAND), 0) == 7
    first_row = iota((EDGE, BAND), 0) == 0

    def outer_slab(g, side):
        sx = side * 2 - 1
        result = []
        for sy in STEPS:
            tap = (sx + 1) * 9 + (sy + 1) * 3
            source = table if sy == 0 else etab.at[side * 2 + (sy + 1) // 2]
            result.append(
                halves(
                    source[index[g, tap + 1]],
                    source[index[g, tap], :, LANES - 128 : LANES],
                    source[index[g, tap + 2], :, 0:128],
                )
            )
        before, same, after = result
        return [
            [
                jnp.where(last_row, before[h], same[h]),
                same[h],
                jnp.where(first_row, after[h], same[h]),
            ]
            for h in range(2)
        ]

    for side in range(2):
        for pair in range(BRICKS // 2):
            even, odd = outer_slab(pair * 2, side), outer_slab(pair * 2 + 1, side)
            for h in range(2):
                for ty in range(3):
                    both = jnp.concatenate([even[h][ty], odd[h][ty]], 0)
                    outer[side, ty, h, pair * 16 : pair * 16 + 16] = both.astype(BF16)
    for side in range(2):
        extra = None
        for ty in range(3):
            first = side * 2 * BAND
            part = jnp.dot(
                outer[side, ty].reshape(2 * FACE, BAND),
                band[ty, first : first + BAND],
                preferred_element_type=F32,
            )
            part = shifted(part, ty)
            extra = part if extra is None else extra + part
        acc[side * 7] = acc[side * 7] + extra.reshape(2, FACE, HALF)

    staged(1, reduced(1, convolved(1)))
    send(1)
    for chunk in range(CHUNKS):
        for steps in straight + turning:
            out_copy(chunk, steps).wait()
        own_copy(chunk).wait()


def hand_over(source, target, held, in_sem, out_sem):
    ins, outs = [], []
    for k, x in enumerate(ORDER):
        ins.append(pltpu.make_async_copy(source.at[:, k], held.at[k], in_sem.at[k]))
        outs.append(pltpu.make_async_copy(held.at[k], target.at[:, x], out_sem.at[k]))
    for copy in ins:
        copy.start()
    for arrived, leaving in zip(ins, outs):
        arrived.wait()
        leaving.start()
    for copy in outs:
        copy.wait()


def shards(features, neighbour_ids, conv_weight, conv_bias, down_weight, coarse_owner):
    size_x = lax.axis_size("bx")
    size_y = lax.axis_size("by")
    slots = 2 * size_y
    hbm_spec = pl.BlockSpec(memory_space=pltpu.HBM)
    out = pl.pallas_call(
        functools.partial(kernel, size_x, size_y),
        out_shape=jax.ShapeDtypeStruct((slots, 4, 4, 4 * CO), BF16),
        in_specs=[hbm_spec] * 6,
        out_specs=pl.BlockSpec(memory_space=pl.ANY),
        scratch_shapes=[
            pltpu.VMEM((BRICKS, 27), jnp.int32),
            pltpu.SMEM((1, BRICKS), jnp.int32),
            pltpu.VMEM((ROWS, LANES), BF16),
            pltpu.VMEM((27, CH, CH), BF16),
            pltpu.VMEM((1, CH), F32),
            pltpu.VMEM((8, CH, CO), BF16),
            pltpu.VMEM((BRICKS, 27), jnp.int32),
            pltpu.SMEM((BRICKS, 27), jnp.int32),
            pltpu.VMEM((4, FACE, LANES), BF16),
            pltpu.VMEM((4, 16, 256), BF16),
            pltpu.VMEM((4, FACE, LANES), BF16),
            pltpu.VMEM((4, 16, 256), BF16),
            pltpu.VMEM((T_SIZE, EDGE, LANES), F32),
            pltpu.VMEM((2, Y_SIZE, EDGE, LANES), F32),
            pltpu.VMEM((4, E_SIZE, EDGE, LANES), F32),
            pltpu.VMEM((10, 2, FACE, BAND), BF16),
            pltpu.VMEM((2, 3, 2, FACE, BAND), BF16),
            pltpu.VMEM((2, 2 * FACE, BAND), BF16),
            pltpu.VMEM((2, 10, 16, BAND), BF16),
            pltpu.VMEM((EDGE, 2, FACE, HALF), F32),
            pltpu.VMEM((3, 3 * BAND, HALF), BF16),
            pltpu.VMEM((256, 2 * CO), BF16),
            pltpu.VMEM((slots * 4 * CHUNK, FACE * CHUNK), BF16),
            pltpu.VMEM((256 * CHUNK, 128 * CHUNK), BF16),
            pltpu.VMEM((CHUNKS, slots, CHUNK, 4, 4 * CO), BF16),
            pltpu.SemaphoreType.DMA((6,)),
            pltpu.SemaphoreType.DMA,
            pltpu.SemaphoreType.DMA((8,)),
            pltpu.SemaphoreType.DMA((8,)),
            pltpu.SemaphoreType.DMA((CHUNKS, size_y)),
            pltpu.SemaphoreType.DMA((CHUNKS, size_y)),
            pltpu.SemaphoreType.DMA((CHUNKS,)),
            pltpu.SemaphoreType.REGULAR,
        ],
        compiler_params=pltpu.CompilerParams(
            collective_id=0, has_side_effects=True, vmem_limit_bytes=63 * 1024 * 1024
        ),
        name="brick_encoder",
    )(
        neighbour_ids,
        coarse_owner.reshape(1, BRICKS),
        features.reshape(ROWS, LANES),
        conv_weight,
        conv_bias.reshape(1, CH),
        down_weight,
    )
    return pl.pallas_call(
        hand_over,
        out_shape=jax.ShapeDtypeStruct(out.shape, out.dtype),
        in_specs=[pl.BlockSpec(memory_space=pl.ANY)],
        out_specs=pl.BlockSpec(memory_space=pl.ANY),
        scratch_shapes=[
            pltpu.VMEM((4, slots, 4, 4 * CO), out.dtype),
            pltpu.SemaphoreType.DMA((4,)),
            pltpu.SemaphoreType.DMA((4,)),
        ],
        compiler_params=pltpu.CompilerParams(vmem_limit_bytes=63 * 1024 * 1024),
        name="hand_over",
    )(out)


def solution(mesh):
    in_specs = (
        P(("bx", "by"), None, None, None),
        P(("bx", "by"), None),
        P(),
        P(),
        P(),
        P(("bx", "by"), None),
    )
    out_specs = P(("bx", "by"), None, None, None)
    return jax.shard_map(shards, mesh=mesh, in_specs=in_specs, out_specs=out_specs, check_vma=False)
```
